256 devices in a mesh: dp: 128 (over z, y_hi, x, core), mp: 2 (over y_lo).
Axes of the slice: x: 4, y: 4 (y_hi: 2, y_lo: 2; y = y_hi * 2 + y_lo), z: 8, core: 2. Of those that a mesh axis runs over, the one named last changes fastest.
Arguments:
- img_emb: bfloat16 [16384, 1152], P(('dp', 'mp')), may hold values from -6 to 6
- txt_emb: bfloat16 [16384, 1152], P('dp'), may hold values from -6 to 6
- logit_scale: float32 [1], replicated, may hold values from 5 to 15
- logit_bias: float32 [1], replicated, may hold values from -2.5 to -0.5
- pos_step: int32 [16384], P(('dp', 'mp')), may hold values from 0 to 7
- pos_row: int32 [16384], P(('dp', 'mp')), may hold values from 0 to 127
- acts: bfloat16 [49152, 1152], P('dp'), may hold values from -6 to 6
- cotangent: bfloat16 [49152, 1152], P('dp'), may hold values from -24 to 24
- w_up: bfloat16 [1152, 2304], P(None, 'mp'), may hold values from -0.1875 to 0.1875
- w_down: bfloat16 [1152, 2304], P(None, 'mp'), may hold values from -0.125 to 0.125
Outputs:
- grad_img: float32 [16384, 1152], P(('dp', 'mp'))
- grad_txt: float32 [16384, 1152], P('dp')
- grad_up: float32 [1152, 2304], P('dp', 'mp')
- grad_down: float32 [1152, 2304], P('dp', 'mp')
- grad_acts: bfloat16 [49152, 1152], P('dp')
The draws below stay inside these ranges and needn't reach their ends.
All inputs are finite; a program needn't handle non-finite values.
Results may differ from the reference program's by a relative error of at most 0.0054.
Values may be sent and summed in bfloat16 or wider, within the bound.
A program may use at most 128 MiB of HBM per device.

```python
from functools import partial
import jax
import jax.numpy as jnp
from jax import lax

D = 1152
FF = 2304
STEPS = 8
B_DEV = 128
A_DEV = 384
B_TOTAL = 16384
A_TOTAL = 49152
N_DP = 128


def touch_ends(drawn, key, least, high):
    longest = drawn.shape.index(max(drawn.shape))
    spots = []
    for shift in (0, 1):
        where = [jax.random.randint(jax.random.fold_in(key, axis), (), 0, length) for axis, length in enumerate(drawn.shape)]
        where[longest] = (where[longest] + shift) % drawn.shape[longest]
        spots.append(tuple(where))
    return drawn.at[spots[0]].set(least).at[spots[1]].set(high)


def spiked(drawn, key, source, target, shards_of, factor):
    owner, partner = [(jnp.arange(drawn.shape[position]) // (drawn.shape[position] // shards_of)).reshape([-1 if axis == position else 1 for axis in range(drawn.ndim)]) for position in (source, target)]
    chosen = jax.random.permutation(key, shards_of)[partner]
    strong = (owner == chosen) | (owner == (partner + shards_of // 2) % shards_of)
    return jnp.where(strong, factor * drawn, drawn)


def shard_levels(rng, shape, split, smallest, top_value):
    gain, own = 1.0, jax.random.fold_in(rng, 6)
    for dim, shards_of in split:
        draws = jnp.exp(jax.random.uniform(jax.random.fold_in(own, dim), (shards_of,), jnp.float32, smallest / len(split), top_value / len(split)))
        gain = gain * jnp.repeat(draws, shape[dim] // shards_of).reshape([-1 if axis == dim else 1 for axis in range(len(shape))])
    return gain


def bell_draw(own_key, extent, width, most, split=(), kind=jnp.bfloat16):
    values = width * jax.random.normal(own_key, extent, jnp.float32)
    if split:
        values = values * shard_levels(own_key, extent, split, -0.22, 0.18)
    return jnp.clip(values, -most, most).astype(kind)


def noise_with(own_key, extent, scale, most, cuts, heavy, held_as=jnp.bfloat16):
    array = scale * jax.random.normal(own_key, extent, jnp.float32)
    if cuts:
        array = array * shard_levels(own_key, extent, cuts, -0.22, 0.18)
    return jnp.clip(spiked(array, jax.random.fold_in(own_key, 3), *heavy), -most, most).astype(held_as)


def setup_inputs(seed: int = 0) -> dict:
    arg_keys = jax.random.split(jax.random.key(seed), 11)
    img_emb = bell_draw(arg_keys[0], (B_TOTAL, D), 1.0, 6.0, ((0, 256),))
    txt_emb = bell_draw(arg_keys[1], (B_TOTAL, D), 1.0, 6.0, ((0, 128),))
    logit_scale = jnp.clip(jax.random.uniform(arg_keys[2], (1,), jnp.float32, 5.0, 15.0), 5.0, 15.0)
    logit_bias = jnp.clip(jax.random.uniform(arg_keys[3], (1,), jnp.float32, -2.5, -0.5), -2.5, -0.5)
    pos_step = touch_ends(jax.random.randint(arg_keys[4], (B_TOTAL,), 0, STEPS), jax.random.fold_in(arg_keys[4], 1), 0, STEPS - 1).astype(jnp.int32)
    pos_row = touch_ends(jax.random.randint(arg_keys[5], (B_TOTAL,), 0, B_DEV), jax.random.fold_in(arg_keys[5], 1), 0, B_DEV - 1).astype(jnp.int32)
    acts = bell_draw(arg_keys[6], (A_TOTAL, D), 1.0, 6.0, ((0, 128),))
    cotangent = noise_with(arg_keys[7], (A_TOTAL, D), 1.0, 24.0, ((0, 128),), (0, 1, 128, 5.5))
    w_up = bell_draw(arg_keys[8], (D, FF), D ** -0.5, 0.1875, ((1, 2),))
    w_down = bell_draw(arg_keys[9], (D, FF), FF ** -0.5, 0.125, ((1, 2),))
    return dict(img_emb=img_emb, txt_emb=txt_emb, logit_scale=logit_scale, logit_bias=logit_bias, pos_step=pos_step, pos_row=pos_row, acts=acts, cotangent=cotangent, w_up=w_up, w_down=w_down)


def unit_rows(values):
    full = values.astype(jnp.float32)
    norms = jnp.sqrt(lax.optimization_barrier(jnp.sum(full * full, axis=-1, keepdims=True)) + 1e-06)
    return (full / norms, norms)

def back_unit(unit, norms, grads):
    return (grads - unit * lax.optimization_barrier(jnp.sum(unit * grads, axis=-1, keepdims=True))) / norms

def reference(img_emb, txt_emb, logit_scale, logit_bias, pos_step, pos_row, acts, cotangent, w_up, w_down):
    scale = logit_scale[0]
    bias = logit_bias[0]
    img_unit, img_norm = unit_rows(img_emb)
    txt_unit, txt_norm = unit_rows(txt_emb)
    img_bf = img_unit.astype(jnp.bfloat16).astype(jnp.float32).reshape(N_DP, B_DEV, D)
    txt_bf = txt_unit.astype(jnp.bfloat16).astype(jnp.float32).reshape(N_DP, B_DEV, D)
    steps_of = pos_step.reshape(N_DP, B_DEV)
    rows_of = pos_row.reshape(N_DP, B_DEV)
    col_ids = jnp.arange(B_DEV, dtype=jnp.int32)
    dimg = jnp.zeros((N_DP, B_DEV, D), jnp.float32)
    dtxt = jnp.zeros((N_DP, B_DEV, D), jnp.float32)
    for step in range(STEPS):
        texts = jnp.roll(txt_bf, step, axis=0)
        logits = scale * jnp.einsum('nbe,nce->nbc', img_bf, texts) + bias
        positive = (steps_of[:, :, None] == step) & (rows_of[:, :, None] == col_ids[None, None, :])
        label = jnp.where(positive, 1.0, -1.0).astype(jnp.float32)
        dlogit = (-label * jax.nn.sigmoid(-label * logits)).astype(jnp.bfloat16).astype(jnp.float32)
        dimg = dimg + jnp.einsum('nbc,nce->nbe', dlogit, texts)
        dtxt = dtxt + jnp.roll(jnp.einsum('nbc,nbe->nce', dlogit, img_bf), -step, axis=0)
    dimg = scale * dimg.reshape(B_TOTAL, D)
    dtxt = scale * dtxt.reshape(B_TOTAL, D)
    grad_img = back_unit(img_unit, img_norm, dimg)
    grad_txt = back_unit(txt_unit, txt_norm, dtxt)
    gelu_fn = partial(jax.nn.gelu, approximate=True)
    blocks_x = acts.reshape(N_DP, A_DEV, D)
    blocks_g = cotangent.reshape(N_DP, A_DEV, D)

    def one_block(carry, pair):
        acc_up, acc_down = carry
        block_x, block_g = pair
        full = block_x.astype(jnp.float32)
        mean = lax.optimization_barrier(jnp.mean(full, axis=-1, keepdims=True))
        centred = full - mean
        rstd = lax.rsqrt(lax.optimization_barrier(jnp.mean(centred * centred, axis=-1, keepdims=True)) + 1e-06)
        normed = centred * rstd
        normed_bf = normed.astype(jnp.bfloat16)
        pre = jnp.dot(normed_bf, w_up, preferred_element_type=jnp.float32)
        hidden_f, gelu_back = jax.vjp(gelu_fn, pre)
        hidden = hidden_f.astype(jnp.bfloat16)
        dhidden = jnp.dot(block_g, w_down, preferred_element_type=jnp.float32)
        dpre = gelu_back(dhidden)[0].astype(jnp.bfloat16)
        acc_up = acc_up + lax.dot_general(normed_bf, dpre, (((0,), (0,)), ((), ())), preferred_element_type=jnp.float32)
        acc_down = acc_down + lax.dot_general(block_g, hidden, (((0,), (0,)), ((), ())), preferred_element_type=jnp.float32)
        dnormed = lax.dot_general(dpre, w_up, (((1,), (1,)), ((), ())), preferred_element_type=jnp.float32)
        inner = dnormed - lax.optimization_barrier(jnp.mean(dnormed, axis=-1, keepdims=True)) - normed * lax.optimization_barrier(jnp.mean(dnormed * normed, axis=-1, keepdims=True))
        grad_block = (block_g.astype(jnp.float32) + rstd * inner).astype(jnp.bfloat16)
        return ((acc_up, acc_down), grad_block)
    zeros = jnp.zeros((D, FF), jnp.float32)
    (grad_up, grad_down), grad_blocks = lax.scan(one_block, (zeros, zeros), (blocks_x, blocks_g))
    return (grad_img, grad_txt, grad_up, grad_down, grad_blocks.reshape(A_TOTAL, D))
```

```python
import jax
import jax.numpy as jnp
from jax import lax
from jax.experimental import pallas as pl
from jax.experimental.pallas import tpu as pltpu
from jax.sharding import PartitionSpec as P

D = 1152
STEPS = 8
IMGS = 64
TXTS = 128
TOK = 384
HALF = 1152
NZ = 8
ZROWS = D // NZ
SUB = 48
NSUB = ZROWS // SUB
WIN = 32
OUT = 9
META = 128
EPS = 1e-06
MESH = pl.DeviceIdType.MESH
F32 = jnp.float32
BF16 = jnp.bfloat16
GELU_C = 0.7978845608028654
GELU_A = 0.044715
TILES = ((0, 256), (256, 256), (512, 256), (768, 256), (1024, 128))


def rows(start, size, align=16):
    return pl.ds(pl.multiple_of(start, align), size)


def nt_dot(a, b):
    return lax.dot_general(a, b, (((1,), (1,)), ((), ())), preferred_element_type=F32)


def tn_dot(a, b):
    return lax.dot_general(a, b, (((0,), (0,)), ((), ())), preferred_element_type=F32)


def nn_dot(a, b):
    return jnp.dot(a, b, preferred_element_type=F32)


def wide_tiles(body):
    @pl.loop(0, 4)
    def _(t):
        body(pl.multiple_of(t * 256, 256), 256)

    body(1024, 128)


def step_kernel(
    scale_ref,
    bias_ref,
    img_h,
    txt_h,
    meta,
    tcol,
    acts_h,
    cot_h,
    wup_h,
    wdn_h,
    gimg,
    gtxt,
    gup,
    gdn,
    gacts,
    img_in,
    txt_in,
    acts,
    cot,
    wup,
    wdn,
    pair_l,
    pair_r,
    left_in,
    right_in,
    normed,
    rstd,
    dnorm,
    grads,
    up_out,
    up_in,
    dn_out,
    dn_in,
    inner_out,
    inner_in,
    zsum,
    zsum_bf,
    win_in,
    fin_out,
    fin_in,
    texts,
    images,
    txt_unit,
    txt_norm,
    img_unit,
    img_norm,
    gt_out,
    gt_in,
    in_sem,
    text_ss,
    text_rs,
    img_ss,
    img_rs,
    pair_ss,
    pair_rs,
    up_ss,
    up_rs,
    dn_ss,
    dn_rs,
    inner_ss,
    inner_rs,
    win_ss,
    win_rs,
    fin_ss,
    fin_rs,
):
    me = lax.axis_index("dp")
    mp = lax.axis_index("mp")
    core = me % 2
    spot = me % 8
    plane = (me // 2) % 8
    zpos = me // 16
    sibling = me + 1 - 2 * core

    def near(shift):
        moved = spot + shift
        crossed = (moved + 8) // 8
        return ((me + shift + 128) % 128, (mp + crossed + 1) % 2)

    def in_plane(turn):
        return ((zpos * 8 + (plane + turn) % 8) * 2 + core, mp)

    special = ((me + 7 * (2 * core - 1) + 128) % 128, (mp + 1) % 2)
    z_up = ((me + 16) % 128, mp)
    z_dn = ((me + 112) % 128, mp)

    loads = [
        pltpu.make_async_copy(source, target, in_sem.at[i])
        for i, (source, target) in enumerate(
            [
                (txt_h, txt_in),
                (img_h, img_in),
                (acts_h, acts),
                (cot_h, cot),
                (wup_h, wup),
                (wdn_h, wdn),
            ]
        )
    ]
    for load in loads:
        load.start()

    barrier = pltpu.get_barrier_semaphore()
    partners = [near(s) for s in (2, 4, 6, -2, -4, -6)]
    partners += [(sibling, mp), special, (me, 1 - mp), z_up, z_dn]
    partners += [in_plane(q) for q in range(1, 8)]
    for partner in partners:
        pl.semaphore_signal(barrier, inc=1, device_id=partner, device_id_type=MESH)

    def send(source, target, send_sem, recv_sem, device):
        copy = pltpu.make_async_remote_copy(
            src_ref=source,
            dst_ref=target,
            send_sem=send_sem,
            recv_sem=recv_sem,
            device_id=device,
            device_id_type=MESH,
        )
        copy.start()
        pending.append(copy)

    def arrived(target, send_sem, recv_sem):
        pltpu.make_async_remote_copy(
            src_ref=target,
            dst_ref=target,
            send_sem=send_sem,
            recv_sem=recv_sem,
            device_id=(sibling, mp),
            device_id_type=MESH,
        ).wait_recv()

    pending = []

    loads[0].wait()

    @pl.loop(0, TXTS // 16)
    def _(i):
        r = rows(i * 16, 16)
        full = txt_in[r, :].astype(F32)
        norm = jnp.sqrt(jnp.sum(full * full, axis=-1, keepdims=True) + EPS)
        unit = full / norm
        txt_unit[r, :] = unit
        txt_norm[r, :] = jnp.broadcast_to(norm, (16, 128))
        texts[0, r, :] = unit.astype(BF16)

    loads[1].wait()

    @pl.loop(0, IMGS // 16)
    def _(i):
        r = rows(i * 16, 16)
        full = img_in[r, :].astype(F32)
        norm = jnp.sqrt(jnp.sum(full * full, axis=-1, keepdims=True) + EPS)
        unit = full / norm
        img_unit[r, :] = unit
        img_norm[r, :] = jnp.broadcast_to(norm, (16, 128))
        images[0, r, 0:D] = unit.astype(BF16)
        images[0, r, D : D + META] = meta[r, :]

    pl.semaphore_wait(barrier, len(partners))

    for i in (1, 2, 3):
        send(texts.at[0], texts.at[2 * i], text_ss.at[i], text_rs.at[i], near(2 * i))
        send(images.at[0], images.at[2 * i], img_ss.at[i], img_rs.at[i], near(-2 * i))
    text_special = (
        (1 - core) * sibling + core * special[0],
        (1 - core) * mp + core * special[1],
    )
    img_special = (
        core * sibling + (1 - core) * special[0],
        core * mp + (1 - core) * special[1],
    )
    send(texts.at[0], texts.at[1 + 6 * core], text_ss.at[0], text_rs.at[0], text_special)
    send(images.at[0], images.at[7 - 6 * core], img_ss.at[0], img_rs.at[0], img_special)

    loads[2].wait()
    loads[3].wait()

    @pl.loop(0, TOK // 16)
    def _(i):
        r = rows(i * 16, 16)
        full = acts[r, :].astype(F32)
        mean = jnp.mean(full, axis=-1, keepdims=True)
        centred = full - mean
        scale = lax.rsqrt(jnp.mean(centred * centred, axis=-1, keepdims=True) + EPS)
        out = centred * scale
        normed[r, :] = out
        rstd[r, :] = jnp.broadcast_to(scale, (16, 128))
        pair_l[core, r, :] = out.astype(BF16)
        pair_l[1 - core, r, :] = cot[r, :]

    send(pair_l.at[1], left_in, pair_ss.at[0], pair_rs.at[0], (sibling, mp))

    loads[4].wait()
    loads[5].wait()

    def hidden_tile(start, width):
        c = pl.ds(start, width)
        pre = nn_dot(pair_l[core, :, :], wup[:, c])
        dhidden = nn_dot(cot[...], wdn[:, c])
        square = pre * pre
        t = jnp.tanh(GELU_C * (pre + GELU_A * (square * pre)))
        half = 0.5 * (1.0 + t)
        slope = half + (0.5 * GELU_C) * pre * (1.0 - t * t) * (1.0 + (3.0 * GELU_A) * square)
        pair_r[1 - core, :, c] = (pre * half).astype(BF16)
        pair_r[core, :, c] = (dhidden * slope).astype(BF16)

    wide_tiles(hidden_tile)
    send(pair_r.at[1], right_in, pair_ss.at[1], pair_rs.at[1], (sibling, mp))

    def dnorm_tile(start, width):
        c = pl.ds(start, width)
        dnorm[:, c] = nt_dot(pair_r[core, :, :], wup[c, :])

    wide_tiles(dnorm_tile)

    @pl.loop(0, TOK // 16)
    def _(i):
        r = rows(i * 16, 16)
        value = dnorm[r, :]
        unit = normed[r, :]
        inner = (
            value
            - jnp.mean(value, axis=-1, keepdims=True)
            - unit * jnp.mean(value * unit, axis=-1, keepdims=True)
        )
        inner_out[r, :] = inner.astype(BF16)

    send(inner_out, inner_in, inner_ss, inner_rs, (me, 1 - mp))

    arrived(left_in, pair_ss.at[0], pair_rs.at[0])
    arrived(right_in, pair_ss.at[1], pair_rs.at[1])

    def grad_tile(start, width):
        c = pl.ds(start, width)
        grads[c, :] = tn_dot(pair_l[0, :, c], pair_r[0, :, :]) + tn_dot(
            left_in[:, c], right_in[...]
        )

    wide_tiles(grad_tile)

    def up_step(s):
        base = ((zpos + 4 - s) % NZ) * ZROWS
        for c in range(NSUB):
            part = pl.ds(c * SUB, SUB)
            value = grads[rows(base + c * SUB, SUB), :]
            if s > 0:
                arrived(up_in.at[s - 1, part], up_ss.at[s - 1, c], up_rs.at[s - 1, c])
                value = value + up_in[s - 1, part, :].astype(F32)
            up_out[s, part, :] = value.astype(BF16)
            send(up_out.at[s, part], up_in.at[s, part], up_ss.at[s, c], up_rs.at[s, c], z_up)

    def dn_step(s):
        base = ((zpos + 5 + s) % NZ) * ZROWS
        for c in range(NSUB):
            part = pl.ds(c * SUB, SUB)
            value = grads[rows(base + c * SUB, SUB), :]
            if s > 0:
                arrived(dn_in.at[s - 1, part], dn_ss.at[s - 1, c], dn_rs.at[s - 1, c])
                value = value + dn_in[s - 1, part, :].astype(F32)
            dn_out[s, part, :] = value.astype(BF16)
            send(dn_out.at[s, part], dn_in.at[s, part], dn_ss.at[s, c], dn_rs.at[s, c], z_dn)

    up_step(0)
    dn_step(0)

    for i in (1, 2, 3):
        arrived(texts.at[2 * i], text_ss.at[i], text_rs.at[i])
        send(
            texts.at[2 * i],
            texts.at[2 * i + 1 - 2 * core],
            text_ss.at[3 + i],
            text_rs.at[3 + i],
            (sibling, mp),
        )
        arrived(images.at[2 * i], img_ss.at[i], img_rs.at[i])
        send(
            images.at[2 * i],
            images.at[2 * i - 1 + 2 * core],
            img_ss.at[3 + i],
            img_rs.at[3 + i],
            (sibling, mp),
        )

    up_step(1)
    dn_step(1)

    arrived(texts.at[7 - 6 * core], text_ss.at[0], text_rs.at[0])
    arrived(images.at[1 + 6 * core], img_ss.at[0], img_rs.at[0])
    for i in (1, 2, 3):
        arrived(texts.at[2 * i - 1 + 2 * core], text_ss.at[3 + i], text_rs.at[3 + i])
        arrived(images.at[2 * i + 1 - 2 * core], img_ss.at[3 + i], img_rs.at[3 + i])

    scale = scale_ref[0]
    bias = bias_ref[0]

    def slope_of(logits, positive):
        label = jnp.where(positive, 1.0, -1.0).astype(F32)
        return (-label * jax.nn.sigmoid(-label * logits)).astype(BF16)

    own_texts = texts[0]
    text_ids = lax.broadcasted_iota(jnp.int32, (TXTS, 128), 0).astype(F32)
    second = (lax.broadcasted_iota(jnp.int32, (TXTS, 128), 1) // IMGS).astype(F32)
    lane_second = lax.broadcasted_iota(jnp.int32, (16, 128), 1) >= IMGS
    dtxt = jnp.zeros((TXTS, D), F32)
    for pair in range(STEPS // 2):
        block = images[2 * pair : 2 * pair + 2, :, 0:D].reshape(2 * IMGS, D)
        logits = scale * nt_dot(own_texts, block) + bias
        first = images[2 * pair, 0:16, D : D + META].astype(F32)
        later = images[2 * pair + 1, 0:16, D : D + META].astype(F32)
        marks = jnp.where(lane_second, later, first)
        target = marks[0:1, :] * float(TXTS) + marks[1:2, :]
        positive = target == (text_ids + (second + float(2 * pair)) * float(TXTS))
        dtxt = dtxt + nn_dot(slope_of(logits, positive), block)
    dtxt = scale * dtxt
    unit = txt_unit[...]
    back = (dtxt - unit * jnp.sum(unit * dtxt, axis=-1, keepdims=True)) / txt_norm[:, 0:1]
    gt_out[...] = back.astype(BF16)
    send(gt_out, gt_in, pair_ss.at[2], pair_rs.at[2], (me, 1 - mp))

    up_step(2)
    dn_step(2)

    own_images = images[0, :, 0:D]
    cols = lax.broadcasted_iota(jnp.int32, (IMGS, TXTS), 1)
    want = tcol[...]
    dimg = jnp.zeros((IMGS, D), F32)
    for k in range(STEPS):
        block = texts[k]
        logits = scale * nt_dot(own_images, block) + bias
        dimg = dimg + nn_dot(slope_of(logits, want == cols + k * TXTS), block)
    dimg = scale * dimg
    unit = img_unit[...]
    gimg[...] = (dimg - unit * jnp.sum(unit * dimg, axis=-1, keepdims=True)) / img_norm[:, 0:1]

    up_step(3)

    arrived(inner_in, inner_ss, inner_rs)

    @pl.loop(0, TOK // 16)
    def _(i):
        r = rows(i * 16, 16)
        both = inner_out[r, :].astype(F32) + inner_in[r, :].astype(F32)
        gacts[r, :] = (cot[r, :].astype(F32) + rstd[r, 0:1] * both).astype(BF16)

    base = zpos * ZROWS
    for c in range(NSUB):
        part = pl.ds(c * SUB, SUB)
        arrived(up_in.at[3, part], up_ss.at[3, c], up_rs.at[3, c])
        arrived(dn_in.at[2, part], dn_ss.at[2, c], dn_rs.at[2, c])
        value = (
            grads[rows(base + c * SUB, SUB), :]
            + up_in[3, part, :].astype(F32)
            + dn_in[2, part, :].astype(F32)
        )
        zsum[part, :] = value
        zsum_bf[part, :] = value.astype(BF16)
    for q in range(1, 8):
        there = (plane + q) % 8
        send(
            zsum_bf.at[rows(there * 16, WIN)],
            win_in.at[q - 1],
            win_ss.at[q - 1],
            win_rs.at[q - 1],
            in_plane(q),
        )

    arrived(gt_in, pair_ss.at[2], pair_rs.at[2])
    gtxt[...] = gt_out[...].astype(F32) + gt_in[...].astype(F32)

    total = zsum[rows(plane * 16, WIN), :]
    for q in range(1, 8):
        arrived(win_in.at[q - 1], win_ss.at[q - 1], win_rs.at[q - 1])
        total = total + win_in[q - 1].astype(F32)
    fin_out[...] = pltpu.roll(total, (2 * WIN - 2 * plane - OUT * (1 - core)) % WIN, 0)[0:16, :]
    send(fin_out, fin_in, fin_ss, fin_rs, (sibling, mp))
    keep = pltpu.roll(total, (2 * WIN - 2 * plane - OUT * core) % WIN, 0)[0:OUT, :]
    arrived(fin_in, fin_ss, fin_rs)
    other = fin_in[0:OUT, :]
    gup[...] = jnp.where(core == 0, keep, other)
    gdn[...] = jnp.where(core == 0, other, keep)

    for copy in pending:
        copy.wait_send()


def shards(
    img_emb, txt_emb, logit_scale, logit_bias, pos_step, pos_row, acts, cotangent, w_up, w_down
):
    marks = jnp.stack([pos_step, pos_row]).astype(BF16)
    meta = jnp.pad(jnp.tile(marks, (1, 2)), ((0, IMGS - 2), (0, 0)))
    tcol = (pos_step * TXTS + pos_row)[:, None]
    vmem = pl.BlockSpec(memory_space=pltpu.VMEM)
    smem = pl.BlockSpec(memory_space=pltpu.SMEM)
    hbm = pl.BlockSpec(memory_space=pl.ANY)
    dma = pltpu.SemaphoreType.DMA
    out = pl.pallas_call(
        step_kernel,
        out_shape=(
            jax.ShapeDtypeStruct((IMGS, D), F32),
            jax.ShapeDtypeStruct((TXTS, D), F32),
            jax.ShapeDtypeStruct((OUT, HALF), F32),
            jax.ShapeDtypeStruct((OUT, HALF), F32),
            jax.ShapeDtypeStruct((TOK, D), BF16),
        ),
        in_specs=[smem, smem, hbm, hbm, vmem, vmem, hbm, hbm, hbm, hbm],
        out_specs=(vmem, vmem, vmem, vmem, vmem),
        scratch_shapes=[
            pltpu.VMEM((IMGS, D), BF16),
            pltpu.VMEM((TXTS, D), BF16),
            pltpu.VMEM((TOK, D), BF16),
            pltpu.VMEM((TOK, D), BF16),
            pltpu.VMEM((D, HALF), BF16),
            pltpu.VMEM((D, HALF), BF16),
            pltpu.VMEM((2, TOK, D), BF16),
            pltpu.VMEM((2, TOK, HALF), BF16),
            pltpu.VMEM((TOK, D), BF16),
            pltpu.VMEM((TOK, HALF), BF16),
            pltpu.VMEM((TOK, D), F32),
            pltpu.VMEM((TOK, 128), F32),
            pltpu.VMEM((TOK, D), F32),
            pltpu.VMEM((D, HALF), F32),
            pltpu.VMEM((4, ZROWS, HALF), BF16),
            pltpu.VMEM((4, ZROWS, HALF), BF16),
            pltpu.VMEM((3, ZROWS, HALF), BF16),
            pltpu.VMEM((3, ZROWS, HALF), BF16),
            pltpu.VMEM((TOK, D), BF16),
            pltpu.VMEM((TOK, D), BF16),
            pltpu.VMEM((ZROWS, HALF), F32),
            pltpu.VMEM((ZROWS, HALF), BF16),
            pltpu.VMEM((7, WIN, HALF), BF16),
            pltpu.VMEM((16, HALF), F32),
            pltpu.VMEM((16, HALF), F32),
            pltpu.VMEM((STEPS, TXTS, D), BF16),
            pltpu.VMEM((STEPS, IMGS, D + META), BF16),
            pltpu.VMEM((TXTS, D), F32),
            pltpu.VMEM((TXTS, 128), F32),
            pltpu.VMEM((IMGS, D), F32),
            pltpu.VMEM((IMGS, 128), F32),
            pltpu.VMEM((TXTS, D), BF16),
            pltpu.VMEM((TXTS, D), BF16),
            dma((6,)),
            dma((7,)),
            dma((7,)),
            dma((7,)),
            dma((7,)),
            dma((3,)),
            dma((3,)),
            dma((4, NSUB)),
            dma((4, NSUB)),
            dma((3, NSUB)),
            dma((3, NSUB)),
            dma,
            dma,
            dma((7,)),
            dma((7,)),
            dma,
            dma,
        ],
        compiler_params=pltpu.CompilerParams(
            collective_id=0, has_side_effects=True, vmem_limit_bytes=58 * 1024 * 1024
        ),
        name="step",
    )(logit_scale, logit_bias, img_emb, txt_emb, meta, tcol, acts, cotangent, w_up, w_down)
    return out


def solution(mesh):
    return jax.shard_map(
        shards,
        mesh=mesh,
        in_specs=(
            P(("dp", "mp"), None),
            P("dp", None),
            P(),
            P(),
            P(("dp", "mp")),
            P(("dp", "mp")),
            P("dp", None),
            P("dp", None),
            P(None, "mp"),
            P(None, "mp"),
        ),
        out_specs=(
            P(("dp", "mp"), None),
            P("dp", None),
            P("dp", "mp"),
            P("dp", "mp"),
            P("dp", None),
        ),
        check_vma=False,
    )
```

```python
import jax
import jax.numpy as jnp
from jax import lax
from jax.experimental import pallas as pl
from jax.experimental.pallas import tpu as pltpu
from jax.sharding import PartitionSpec as P

D = 1152
STEPS = 8
IMGS = 64
TXTS = 128
HTXT = 64
TOK = 384
HALF = 1152
NZ = 8
ZROWS = D // NZ
SUB = 48
NSUB = ZROWS // SUB
WIN = 32
OUT = 9
META = 128
LN = 64
EPS = 1e-06
MESH = pl.DeviceIdType.MESH
F32 = jnp.float32
BF16 = jnp.bfloat16
GELU_C = 0.7978845608028654
GELU_A = 0.044715
TILES = ((0, 256), (256, 256), (512, 256), (768, 256), (1024, 128))


def rows(start, size, align=16):
    return pl.ds(pl.multiple_of(start, align), size)


def nt_dot(a, b):
    return lax.dot_general(a, b, (((1,), (1,)), ((), ())), preferred_element_type=F32)


def tn_dot(a, b):
    return lax.dot_general(a, b, (((0,), (0,)), ((), ())), preferred_element_type=F32)


def nn_dot(a, b):
    return jnp.dot(a, b, preferred_element_type=F32)


def wide_tiles(body):
    @pl.loop(0, 4)
    def _(t):
        body(pl.multiple_of(t * 256, 256), 256)

    body(1024, 128)


def step_kernel(
    scale_ref,
    bias_ref,
    img_h,
    txt_h,
    pstep,
    prow,
    acts_h,
    cot_h,
    wup_h,
    wdn_h,
    gimg,
    gtxt,
    gup,
    gdn,
    gacts,
    img_in,
    txt_in,
    acts,
    cot,
    wup,
    wdn,
    pair_l,
    pair_r,
    left_in,
    right_in,
    normed,
    rstd,
    dnorm,
    grads,
    up_out,
    up_in,
    dn_out,
    dn_in,
    inner_out,
    inner_in,
    zsum,
    zsum_bf,
    win_in,
    fin_out,
    fin_in,
    own_texts,
    texts,
    images,
    img_too,
    both,
    txt_unit,
    txt_norm,
    img_unit,
    img_norm,
    gt_out,
    gt_in,
    gi_out,
    gi_in,
    in_sem,
    text_ss,
    text_rs,
    img_ss,
    img_rs,
    pair_ss,
    pair_rs,
    up_ss,
    up_rs,
    dn_ss,
    dn_rs,
    inner_ss,
    inner_rs,
    win_ss,
    win_rs,
    fin_ss,
    fin_rs,
):
    me = lax.axis_index("dp")
    mp = lax.axis_index("mp")
    core = me % 2
    spot = me % 8
    plane = (me // 2) % 8
    zpos = me // 16
    sibling = me + 1 - 2 * core

    def near(shift):
        moved = spot + shift
        crossed = (moved + 8) // 8
        return ((me + shift + 128) % 128, (mp + crossed + 1) % 2)

    def in_plane(turn):
        return ((zpos * 8 + (plane + turn) % 8) * 2 + core, mp)

    special = ((me + 7 * (2 * core - 1) + 128) % 128, (mp + 1) % 2)
    z_up = ((me + 16) % 128, mp)
    z_dn = ((me + 112) % 128, mp)

    loads = [
        pltpu.make_async_copy(source, target, in_sem.at[i])
        for i, (source, target) in enumerate(
            [
                (txt_h, txt_in),
                (img_h, img_in.at[:, pl.ds(0, D)]),
                (acts_h, acts),
                (cot_h, cot),
                (wup_h, wup),
                (wdn_h, wdn),
            ]
        )
    ]
    for load in loads:
        load.start()

    barrier = pltpu.get_barrier_semaphore()
    partners = [near(s) for s in (2, 4, 6, -2, -4, -6)]
    partners += [(sibling, mp), special, (me, 1 - mp), z_up, z_dn]
    partners += [in_plane(q) for q in range(1, 8)]
    for partner in partners:
        pl.semaphore_signal(barrier, inc=1, device_id=partner, device_id_type=MESH)

    def send(source, target, send_sem, recv_sem, device):
        copy = pltpu.make_async_remote_copy(
            src_ref=source,
            dst_ref=target,
            send_sem=send_sem,
            recv_sem=recv_sem,
            device_id=device,
            device_id_type=MESH,
        )
        copy.start()
        pending.append(copy)

    def arrived(target, send_sem, recv_sem):
        pltpu.make_async_remote_copy(
            src_ref=target,
            dst_ref=target,
            send_sem=send_sem,
            recv_sem=recv_sem,
            device_id=(sibling, mp),
            device_id_type=MESH,
        ).wait_recv()

    pending = []

    loads[0].wait()

    @pl.loop(0, TXTS // LN)
    def _(i):
        r = rows(i * LN, LN)
        full = txt_in[r, :].astype(F32)
        norm = jnp.sqrt(jnp.sum(full * full, axis=-1, keepdims=True) + EPS)
        unit = full / norm
        txt_unit[r, :] = unit
        txt_norm[r, :] = jnp.broadcast_to(norm, (LN, 128))
        own_texts[r, :] = unit.astype(BF16)

    loads[1].wait()

    @pl.loop(0, IMGS // LN)
    def _(i):
        r = rows(i * LN, LN)
        full = img_in[r, 0:D].astype(F32)
        norm = jnp.sqrt(jnp.sum(full * full, axis=-1, keepdims=True) + EPS)
        unit = full / norm
        img_unit[r, :] = unit
        img_norm[r, :] = jnp.broadcast_to(norm, (LN, 128))
        images[0, r, 0:D] = unit.astype(BF16)

    texts[0] = own_texts[rows(mp * HTXT, HTXT), :]

    mark_row = lax.broadcasted_iota(jnp.int32, (IMGS, IMGS), 0)
    mark_col = lax.broadcasted_iota(jnp.int32, (IMGS, IMGS), 1)
    marks = jnp.where(mark_row == 0, pstep[...], prow[...]).astype(F32).astype(BF16)
    for place in (0, IMGS):
        images[0, :, D + place : D + place + IMGS] = marks
        img_in[:, D + place : D + place + IMGS] = marks

    loads[2].wait()
    loads[3].wait()

    @pl.loop(0, TOK // LN)
    def _(i):
        r = rows(i * LN, LN)
        full = acts[r, :].astype(F32)
        mean = jnp.mean(full, axis=-1, keepdims=True)
        centred = full - mean
        scale = lax.rsqrt(jnp.mean(centred * centred, axis=-1, keepdims=True) + EPS)
        out = centred * scale
        normed[r, :] = out
        rstd[r, :] = jnp.broadcast_to(scale, (LN, 128))
        pair_l[core, r, :] = out.astype(BF16)
        pair_l[1 - core, r, :] = cot[r, :]

    pl.semaphore_wait(barrier, len(partners))

    send(pair_l.at[1], left_in, pair_ss.at[0], pair_rs.at[0], (sibling, mp))

    send(img_in, img_too, pair_ss.at[3], pair_rs.at[3], (me, 1 - mp))
    for i in (1, 3, 2):
        send(texts.at[0], texts.at[2 * i], text_ss.at[i], text_rs.at[i], near(2 * i))
        send(images.at[0], images.at[2 * i], img_ss.at[i], img_rs.at[i], near(-2 * i))
    text_special = (
        (1 - core) * sibling + core * special[0],
        (1 - core) * mp + core * special[1],
    )
    img_special = (
        core * sibling + (1 - core) * special[0],
        core * mp + (1 - core) * special[1],
    )
    send(texts.at[0], texts.at[1 + 6 * core], text_ss.at[0], text_rs.at[0], text_special)
    send(images.at[0], images.at[7 - 6 * core], img_ss.at[0], img_rs.at[0], img_special)

    loads[4].wait()
    loads[5].wait()

    def hidden_tile(start, width):
        c = pl.ds(start, width)
        pre = nn_dot(pair_l[core, :, :], wup[:, c])
        dhidden = nn_dot(cot[...], wdn[:, c])
        square = pre * pre
        t = jnp.tanh(GELU_C * (pre + GELU_A * (square * pre)))
        half = 0.5 * (1.0 + t)
        slope = half + (0.5 * GELU_C) * pre * (1.0 - t * t) * (1.0 + (3.0 * GELU_A) * square)
        pair_r[1 - core, :, c] = (pre * half).astype(BF16)
        pair_r[core, :, c] = (dhidden * slope).astype(BF16)

    wide_tiles(hidden_tile)
    send(pair_r.at[1], right_in, pair_ss.at[1], pair_rs.at[1], (sibling, mp))

    arrived(left_in, pair_ss.at[0], pair_rs.at[0])
    arrived(right_in, pair_ss.at[1], pair_rs.at[1])

    def grad_tile(start, width):
        c = pl.ds(start, width)
        grads[c, :] = tn_dot(pair_l[0, :, c], pair_r[0, :, :]) + tn_dot(
            left_in[:, c], right_in[...]
        )

    wide_tiles(grad_tile)

    def hop(s, c, shift, out, came, ss, rs, device):
        base = ((zpos + shift) % NZ) * ZROWS
        part = pl.ds(c * SUB, SUB)
        value = grads[rows(base + c * SUB, SUB), :]
        if s > 0:
            arrived(came.at[s - 1, part], ss.at[s - 1, c], rs.at[s - 1, c])
            value = value + came[s - 1, part, :].astype(F32)
        out[s, part, :] = value.astype(BF16)
        send(out.at[s, part], came.at[s, part], ss.at[s, c], rs.at[s, c], device)

    def z_step(s):
        for c in range(NSUB):
            hop(s, c, 4 - s, up_out, up_in, up_ss, up_rs, z_up)
            if s < 3:
                hop(s, c, 5 + s, dn_out, dn_in, dn_ss, dn_rs, z_dn)

    z_step(0)

    def dnorm_tile(start, width):
        c = pl.ds(start, width)
        dnorm[:, c] = nt_dot(pair_r[core, :, :], wup[c, :])

    wide_tiles(dnorm_tile)

    @pl.loop(0, TOK // LN)
    def _(i):
        r = rows(i * LN, LN)
        value = dnorm[r, :]
        unit = normed[r, :]
        inner = (
            value
            - jnp.mean(value, axis=-1, keepdims=True)
            - unit * jnp.mean(value * unit, axis=-1, keepdims=True)
        )
        inner_out[r, :] = inner.astype(BF16)

    send(inner_out, inner_in, inner_ss, inner_rs, (me, 1 - mp))

    z_step(1)

    z_step(2)

    for i in (1, 2, 3):
        arrived(texts.at[2 * i], text_ss.at[i], text_rs.at[i])
        send(
            texts.at[2 * i],
            texts.at[2 * i + 1 - 2 * core],
            text_ss.at[3 + i],
            text_rs.at[3 + i],
            (sibling, mp),
        )
        arrived(images.at[2 * i], img_ss.at[i], img_rs.at[i])
        send(
            images.at[2 * i],
            images.at[2 * i - 1 + 2 * core],
            img_ss.at[3 + i],
            img_rs.at[3 + i],
            (sibling, mp),
        )

    z_step(3)

    arrived(texts.at[7 - 6 * core], text_ss.at[0], text_rs.at[0])
    arrived(images.at[1 + 6 * core], img_ss.at[0], img_rs.at[0])
    for i in (1, 2, 3):
        arrived(texts.at[2 * i - 1 + 2 * core], text_ss.at[3 + i], text_rs.at[3 + i])
        arrived(images.at[2 * i + 1 - 2 * core], img_ss.at[3 + i], img_rs.at[3 + i])

    scale = scale_ref[0]
    bias = bias_ref[0]

    def slope_of(logits, positive):
        label = jnp.where(positive, 1.0, -1.0).astype(F32)
        return (-label * jax.nn.sigmoid(-label * logits)).astype(BF16)

    def target_of(marked):
        return marked[0:1, :] * float(TXTS) + marked[1:2, :]

    def project(value, unit, norm):
        return (value - unit * jnp.sum(unit * value, axis=-1, keepdims=True)) / norm

    words = own_texts[...]
    text_ids = lax.broadcasted_iota(jnp.int32, (TXTS, 128), 0).astype(F32)
    second = (lax.broadcasted_iota(jnp.int32, (TXTS, 128), 1) // IMGS).astype(F32)
    lane_second = lax.broadcasted_iota(jnp.int32, (16, 128), 1) >= IMGS
    dtxt = jnp.zeros((TXTS, D), F32)
    for pair in range(STEPS // 2):
        block = images[2 * pair : 2 * pair + 2, :, 0:D].reshape(2 * IMGS, D)
        logits = scale * nt_dot(words, block) + bias
        first = images[2 * pair, 0:16, D : D + META].astype(F32)
        later = images[2 * pair + 1, 0:16, D : D + META].astype(F32)
        target = target_of(jnp.where(lane_second, later, first))
        positive = target == (text_ids + (second + float(2 * pair)) * float(TXTS))
        dtxt = dtxt + nn_dot(slope_of(logits, positive), block)
    gt_out[...] = project(scale * dtxt, txt_unit[...], txt_norm[:, 0:1]).astype(BF16)
    send(gt_out, gt_in, pair_ss.at[2], pair_rs.at[2], (me, 1 - mp))

    arrived(img_too, pair_ss.at[3], pair_rs.at[3])
    full = img_too[:, 0:D].astype(F32)
    norm = jnp.sqrt(jnp.sum(full * full, axis=-1, keepdims=True) + EPS)
    unit = full / norm
    img_unit[IMGS:, :] = unit
    img_norm[IMGS:, :] = jnp.broadcast_to(norm, (IMGS, 128))
    both[0:IMGS, :] = images[0, :, 0:D]
    both[IMGS:, :] = unit.astype(BF16)

    def as_column(marked):
        line = target_of(marked.astype(F32))[:, 0:IMGS]
        return jnp.sum(jnp.where(mark_row == mark_col, line, 0.0), axis=-1, keepdims=True)

    want = jnp.concatenate(
        [as_column(img_in[0:16, D : D + META]), as_column(img_too[0:16, D : D + META])], axis=0
    )
    lane = lax.broadcasted_iota(jnp.int32, (2 * IMGS, 2 * HTXT), 1)
    pictures = both[...]
    dimg = jnp.zeros((2 * IMGS, D), F32)
    for pair in range(STEPS // 2):
        block = texts[2 * pair : 2 * pair + 2].reshape(2 * HTXT, D)
        starts = [k * TXTS + near(-k)[1] * HTXT for k in (2 * pair, 2 * pair + 1)]
        column = jnp.where(lane < HTXT, lane + starts[0], lane + (starts[1] - HTXT))
        logits = scale * nt_dot(pictures, block) + bias
        dimg = dimg + nn_dot(slope_of(logits, want == column.astype(F32)), block)
    dimg = project(scale * dimg, img_unit[...], img_norm[:, 0:1])
    gimg[...] = dimg[0:IMGS, :]
    gi_out[...] = dimg[IMGS:, :].astype(BF16)
    send(gi_out, gi_in, pair_ss.at[4], pair_rs.at[4], (me, 1 - mp))

    arrived(inner_in, inner_ss, inner_rs)

    @pl.loop(0, TOK // LN)
    def _(i):
        r = rows(i * LN, LN)
        total = inner_out[r, :].astype(F32) + inner_in[r, :].astype(F32)
        gacts[r, :] = (cot[r, :].astype(F32) + rstd[r, 0:1] * total).astype(BF16)

    base = zpos * ZROWS
    for c in range(NSUB):
        part = pl.ds(c * SUB, SUB)
        arrived(up_in.at[3, part], up_ss.at[3, c], up_rs.at[3, c])
        arrived(dn_in.at[2, part], dn_ss.at[2, c], dn_rs.at[2, c])
        value = (
            grads[rows(base + c * SUB, SUB), :]
            + up_in[3, part, :].astype(F32)
            + dn_in[2, part, :].astype(F32)
        )
        zsum[part, :] = value
        zsum_bf[part, :] = value.astype(BF16)
    for q in range(1, 8):
        there = (plane + q) % 8
        send(
            zsum_bf.at[rows(there * 16, WIN)],
            win_in.at[q - 1],
            win_ss.at[q - 1],
            win_rs.at[q - 1],
            in_plane(q),
        )

    arrived(gt_in, pair_ss.at[2], pair_rs.at[2])
    gtxt[...] = gt_out[...].astype(F32) + gt_in[...].astype(F32)
    arrived(gi_in, pair_ss.at[4], pair_rs.at[4])
    gimg[...] = gimg[...] + gi_in[...].astype(F32)

    total = zsum[rows(plane * 16, WIN), :]
    for q in range(1, 8):
        arrived(win_in.at[q - 1], win_ss.at[q - 1], win_rs.at[q - 1])
        total = total + win_in[q - 1].astype(F32)
    fin_out[...] = pltpu.roll(total, (2 * WIN - 2 * plane - OUT * (1 - core)) % WIN, 0)[0:16, :]
    send(fin_out, fin_in, fin_ss, fin_rs, (sibling, mp))
    keep = pltpu.roll(total, (2 * WIN - 2 * plane - OUT * core) % WIN, 0)[0:OUT, :]
    arrived(fin_in, fin_ss, fin_rs)
    other = fin_in[0:OUT, :]
    gup[...] = jnp.where(core == 0, keep, other)
    gdn[...] = jnp.where(core == 0, other, keep)

    for copy in pending:
        copy.wait_send()


def hand_over(*refs):
    for i in range(5):
        refs[5 + i][...] = refs[i][...]


def shards(
    img_emb, txt_emb, logit_scale, logit_bias, pos_step, pos_row, acts, cotangent, w_up, w_down
):
    pstep = pos_step.reshape(1, IMGS)
    prow = pos_row.reshape(1, IMGS)
    vmem = pl.BlockSpec(memory_space=pltpu.VMEM)
    smem = pl.BlockSpec(memory_space=pltpu.SMEM)
    hbm = pl.BlockSpec(memory_space=pl.ANY)
    dma = pltpu.SemaphoreType.DMA
    out = pl.pallas_call(
        step_kernel,
        out_shape=(
            jax.ShapeDtypeStruct((IMGS, D), F32),
            jax.ShapeDtypeStruct((TXTS, D), F32),
            jax.ShapeDtypeStruct((OUT, HALF), F32),
            jax.ShapeDtypeStruct((OUT, HALF), F32),
            jax.ShapeDtypeStruct((TOK, D), BF16),
        ),
        in_specs=[smem, smem, hbm, hbm, vmem, vmem, hbm, hbm, hbm, hbm],
        out_specs=(vmem, vmem, vmem, vmem, vmem),
        scratch_shapes=[
            pltpu.VMEM((IMGS, D + META), BF16),
            pltpu.VMEM((TXTS, D), BF16),
            pltpu.VMEM((TOK, D), BF16),
            pltpu.VMEM((TOK, D), BF16),
            pltpu.VMEM((D, HALF), BF16),
            pltpu.VMEM((D, HALF), BF16),
            pltpu.VMEM((2, TOK, D), BF16),
            pltpu.VMEM((2, TOK, HALF), BF16),
            pltpu.VMEM((TOK, D), BF16),
            pltpu.VMEM((TOK, HALF), BF16),
            pltpu.VMEM((TOK, D), F32),
            pltpu.VMEM((TOK, 128), F32),
            pltpu.VMEM((TOK, D), F32),
            pltpu.VMEM((D, HALF), F32),
            pltpu.VMEM((4, ZROWS, HALF), BF16),
            pltpu.VMEM((4, ZROWS, HALF), BF16),
            pltpu.VMEM((3, ZROWS, HALF), BF16),
            pltpu.VMEM((3, ZROWS, HALF), BF16),
            pltpu.VMEM((TOK, D), BF16),
            pltpu.VMEM((TOK, D), BF16),
            pltpu.VMEM((ZROWS, HALF), F32),
            pltpu.VMEM((ZROWS, HALF), BF16),
            pltpu.VMEM((7, WIN, HALF), BF16),
            pltpu.VMEM((16, HALF), F32),
            pltpu.VMEM((16, HALF), F32),
            pltpu.VMEM((TXTS, D), BF16),
            pltpu.VMEM((STEPS, HTXT, D), BF16),
            pltpu.VMEM((STEPS, IMGS, D + META), BF16),
            pltpu.VMEM((IMGS, D + META), BF16),
            pltpu.VMEM((2 * IMGS, D), BF16),
            pltpu.VMEM((TXTS, D), F32),
            pltpu.VMEM((TXTS, 128), F32),
            pltpu.VMEM((2 * IMGS, D), F32),
            pltpu.VMEM((2 * IMGS, 128), F32),
            pltpu.VMEM((TXTS, D), BF16),
            pltpu.VMEM((TXTS, D), BF16),
            pltpu.VMEM((IMGS, D), BF16),
            pltpu.VMEM((IMGS, D), BF16),
            dma((6,)),
            dma((7,)),
            dma((7,)),
            dma((7,)),
            dma((7,)),
            dma((5,)),
            dma((5,)),
            dma((4, NSUB)),
            dma((4, NSUB)),
            dma((3, NSUB)),
            dma((3, NSUB)),
            dma,
            dma,
            dma((7,)),
            dma((7,)),
            dma,
            dma,
        ],
        compiler_params=pltpu.CompilerParams(
            collective_id=0, has_side_effects=True, vmem_limit_bytes=58 * 1024 * 1024
        ),
        name="step",
    )(logit_scale, logit_bias, img_emb, txt_emb, pstep, prow, acts, cotangent, w_up, w_down)
    return pl.pallas_call(
        hand_over,
        out_shape=tuple(jax.ShapeDtypeStruct(x.shape, x.dtype) for x in out),
        in_specs=[vmem] * 5,
        out_specs=(vmem,) * 5,
        name="hand_over",
    )(*out)


def solution(mesh):
    return jax.shard_map(
        shards,
        mesh=mesh,
        in_specs=(
            P(("dp", "mp"), None),
            P("dp", None),
            P(),
            P(),
            P(("dp", "mp")),
            P(("dp", "mp")),
            P("dp", None),
            P("dp", None),
            P(None, "mp"),
            P(None, "mp"),
        ),
        out_specs=(
            P(("dp", "mp"), None),
            P("dp", None),
            P("dp", "mp"),
            P("dp", "mp"),
            P("dp", None),
        ),
        check_vma=False,
    )
```

```python
import jax
import jax.numpy as jnp
from jax import lax
from jax.experimental import pallas as pl
from jax.experimental.pallas import tpu as pltpu
from jax.sharding import PartitionSpec as P

D = 1152
STEPS = 8
IMGS = 64
TXTS = 128
HTXT = 64
TOK = 384
HALF = 1152
NZ = 8
ZROWS = D // NZ
SUB = 48
NSUB = ZROWS // SUB
CZ = 768
CX = HALF - CZ
NX = 4
HWIN = 24
ZWIN = 2 * HWIN
XROWS = NZ * ZWIN
XSUB = 2 * ZWIN
NXSUB = XROWS // XSUB
WIN = 32
OUT = 9
META = 128
LN = 64
EPS = 1e-06
MESH = pl.DeviceIdType.MESH
F32 = jnp.float32
BF16 = jnp.bfloat16
GELU_C = 0.7978845608028654
GELU_A = 0.044715
TILES = ((0, 256), (256, 256), (512, 256), (768, 256), (1024, 128))


def rows(start, size, align=16):
    return pl.ds(pl.multiple_of(start, align), size)


def nt_dot(a, b):
    return lax.dot_general(a, b, (((1,), (1,)), ((), ())), preferred_element_type=F32)


def tn_dot(a, b):
    return lax.dot_general(a, b, (((0,), (0,)), ((), ())), preferred_element_type=F32)


def nn_dot(a, b):
    return jnp.dot(a, b, preferred_element_type=F32)


def wide_tiles(body):
    @pl.loop(0, 4)
    def _(t):
        body(pl.multiple_of(t * 256, 256), 256)

    body(1024, 128)


def step_kernel(
    scale_ref,
    bias_ref,
    img_h,
    txt_h,
    pstep,
    prow,
    acts_h,
    cot_h,
    wup_h,
    wdn_h,
    gimg,
    gtxt,
    gup,
    gdn,
    gacts,
    img_in,
    txt_in,
    acts,
    cot,
    wup,
    wdn,
    pair_l,
    pair_r,
    left_in,
    right_in,
    normed,
    rstd,
    dnorm,
    grads,
    up_out,
    up_in,
    dn_out,
    dn_in,
    inner_out,
    inner_in,
    xd_out,
    xd_in,
    xu_out,
    xu_in,
    zsum,
    zsum_bf,
    xsum,
    xsum_bf,
    win_in,
    zwin_in,
    y_out,
    y_in,
    fin_out,
    fin_in,
    own_texts,
    texts,
    images,
    img_too,
    both,
    txt_unit,
    txt_norm,
    img_unit,
    img_norm,
    gt_out,
    gt_in,
    gi_out,
    gi_in,
    in_sem,
    text_ss,
    text_rs,
    img_ss,
    img_rs,
    pair_ss,
    pair_rs,
    up_ss,
    up_rs,
    dn_ss,
    dn_rs,
    inner_ss,
    inner_rs,
    xd_ss,
    xd_rs,
    xu_ss,
    xu_rs,
    win_ss,
    win_rs,
    zwin_ss,
    zwin_rs,
    y_ss,
    y_rs,
    fin_ss,
    fin_rs,
):
    me = lax.axis_index("dp")
    mp = lax.axis_index("mp")
    core = me % 2
    spot = me % 8
    plane = (me // 2) % 8
    zpos = me // 16
    sibling = me + 1 - 2 * core

    def near(shift):
        moved = spot + shift
        crossed = (moved + 8) // 8
        return ((me + shift + 128) % 128, (mp + crossed + 1) % 2)

    def in_plane(turn):
        return ((zpos * 8 + (plane + turn) % 8) * 2 + core, mp)

    special = ((me + 7 * (2 * core - 1) + 128) % 128, (mp + 1) % 2)
    xpos = plane % 4
    half = plane // 4
    x_up = (me + 2 * ((xpos + 1) % 4 - xpos), mp)
    x_dn = (me + 2 * ((xpos + 3) % 4 - xpos), mp)

    def along_z(turn):
        return ((me + 16 * turn) % 128, mp)

    z_up = along_z(1)
    z_dn = along_z(7)

    def load(source, target, i):
        copy = pltpu.make_async_copy(source, target, in_sem.at[i])
        copy.start()
        return copy

    acts_load = load(acts_h, acts, 0)
    txt_load = load(txt_h, txt_in, 1)
    img_load = load(img_h, img_in.at[:, pl.ds(0, D)], 2)
    wup_load = load(wup_h, wup, 3)
    cot_load = load(cot_h, cot, 4)
    wdn_load = load(wdn_h, wdn, 5)

    barrier = pltpu.get_barrier_semaphore()
    partners = [near(s) for s in (2, 4, 6, -2, -4, -6)]
    partners += [(sibling, mp), special, (me, 1 - mp)]
    partners += [along_z(q) for q in range(1, 8)]
    partners += [in_plane(q) for q in range(1, 8)]
    for partner in partners:
        pl.semaphore_signal(barrier, inc=1, device_id=partner, device_id_type=MESH)

    def send(source, target, send_sem, recv_sem, device):
        copy = pltpu.make_async_remote_copy(
            src_ref=source,
            dst_ref=target,
            send_sem=send_sem,
            recv_sem=recv_sem,
            device_id=device,
            device_id_type=MESH,
        )
        copy.start()
        pending.append(copy)

    def arrived(target, send_sem, recv_sem):
        pltpu.make_async_remote_copy(
            src_ref=target,
            dst_ref=target,
            send_sem=send_sem,
            recv_sem=recv_sem,
            device_id=(sibling, mp),
            device_id_type=MESH,
        ).wait_recv()

    pending = []

    txt_load.wait()

    @pl.loop(0, TXTS // LN)
    def _(i):
        r = rows(i * LN, LN)
        full = txt_in[r, :].astype(F32)
        norm = jnp.sqrt(jnp.sum(full * full, axis=-1, keepdims=True) + EPS)
        unit = full / norm
        txt_unit[r, :] = unit
        txt_norm[r, :] = jnp.broadcast_to(norm, (LN, 128))
        own_texts[r, :] = unit.astype(BF16)

    img_load.wait()

    @pl.loop(0, IMGS // LN)
    def _(i):
        r = rows(i * LN, LN)
        full = img_in[r, 0:D].astype(F32)
        norm = jnp.sqrt(jnp.sum(full * full, axis=-1, keepdims=True) + EPS)
        unit = full / norm
        img_unit[r, :] = unit
        img_norm[r, :] = jnp.broadcast_to(norm, (LN, 128))
        images[0, r, 0:D] = unit.astype(BF16)

    texts[0] = own_texts[rows(mp * HTXT, HTXT), :]

    mark_row = lax.broadcasted_iota(jnp.int32, (IMGS, IMGS), 0)
    mark_col = lax.broadcasted_iota(jnp.int32, (IMGS, IMGS), 1)
    marks = jnp.where(mark_row == 0, pstep[...], prow[...]).astype(F32).astype(BF16)
    for place in (0, IMGS):
        images[0, :, D + place : D + place + IMGS] = marks
        img_in[:, D + place : D + place + IMGS] = marks

    acts_load.wait()

    @pl.loop(0, TOK // LN)
    def _(i):
        r = rows(i * LN, LN)
        full = acts[r, :].astype(F32)
        mean = jnp.mean(full, axis=-1, keepdims=True)
        centred = full - mean
        scale = lax.rsqrt(jnp.mean(centred * centred, axis=-1, keepdims=True) + EPS)
        out = centred * scale
        normed[r, :] = out
        rstd[r, :] = jnp.broadcast_to(scale, (LN, 128))
        pair_l[core, r, :] = out.astype(BF16)

    cot_load.wait()

    @pl.loop(0, TOK // LN)
    def _(i):
        r = rows(i * LN, LN)
        pair_l[1 - core, r, :] = cot[r, :]

    pl.semaphore_wait(barrier, len(partners))

    send(pair_l.at[1], left_in, pair_ss.at[0], pair_rs.at[0], (sibling, mp))

    send(img_in, img_too, pair_ss.at[3], pair_rs.at[3], (me, 1 - mp))
    for i in (1, 3, 2):
        send(texts.at[0], texts.at[2 * i], text_ss.at[i], text_rs.at[i], near(2 * i))
        send(images.at[0], images.at[2 * i], img_ss.at[i], img_rs.at[i], near(-2 * i))
    text_special = (
        (1 - core) * sibling + core * special[0],
        (1 - core) * mp + core * special[1],
    )
    img_special = (
        core * sibling + (1 - core) * special[0],
        core * mp + (1 - core) * special[1],
    )
    send(texts.at[0], texts.at[1 + 6 * core], text_ss.at[0], text_rs.at[0], text_special)
    send(images.at[0], images.at[7 - 6 * core], img_ss.at[0], img_rs.at[0], img_special)

    wup_load.wait()
    wdn_load.wait()

    def hidden_tile(start, width):
        c = pl.ds(start, width)
        pre = nn_dot(pair_l[core, :, :], wup[:, c])
        dhidden = nn_dot(cot[...], wdn[:, c])
        square = pre * pre
        t = jnp.tanh(GELU_C * (pre + GELU_A * (square * pre)))
        half = 0.5 * (1.0 + t)
        slope = half + (0.5 * GELU_C) * pre * (1.0 - t * t) * (1.0 + (3.0 * GELU_A) * square)
        pair_r[1 - core, :, c] = (pre * half).astype(BF16)
        pair_r[core, :, c] = (dhidden * slope).astype(BF16)

    wide_tiles(hidden_tile)

    send(pair_r.at[1], right_in, pair_ss.at[1], pair_rs.at[1], (sibling, mp))

    def dnorm_tile(start, width):
        c = pl.ds(start, width)
        dnorm[:, c] = nt_dot(pair_r[core, :, :], wup[c, :])

    wide_tiles(dnorm_tile)

    @pl.loop(0, TOK // LN)
    def _(i):
        r = rows(i * LN, LN)
        value = dnorm[r, :]
        unit = normed[r, :]
        inner = (
            value
            - jnp.mean(value, axis=-1, keepdims=True)
            - unit * jnp.mean(value * unit, axis=-1, keepdims=True)
        )
        inner_out[r, :] = inner.astype(BF16)

    send(inner_out, inner_in, inner_ss, inner_rs, (me, 1 - mp))

    arrived(left_in, pair_ss.at[0], pair_rs.at[0])
    arrived(right_in, pair_ss.at[1], pair_rs.at[1])

    def grad_tile(start, width):
        c = pl.ds(start, width)
        grads[c, :] = tn_dot(pair_l[0, :, c], pair_r[0]) + tn_dot(left_in[:, c], right_in[...])

    wide_tiles(grad_tile)

    def hop(s, c, shift, out, came, ss, rs, device):
        base = ((zpos + shift) % NZ) * ZROWS
        part = pl.ds(c * SUB, SUB)
        value = grads[rows(base + c * SUB, SUB), 0:CZ]
        if s > 0:
            arrived(came.at[s - 1, part], ss.at[s - 1, c], rs.at[s - 1, c])
            value = value + came[s - 1, part, :].astype(F32)
        out[s, part, :] = value.astype(BF16)
        send(out.at[s, part], came.at[s, part], ss.at[s, c], rs.at[s, c], device)

    def x_term(shift, c):
        there = (xpos + shift) % NX
        return jnp.concatenate(
            [
                grads[rows(144 * z + 72 * h + 16 * there, HWIN, 8), CZ:]
                for z in (2 * c, 2 * c + 1)
                for h in (0, 1)
            ],
            axis=0,
        )

    def x_hop(s, c, shift, out, came, ss, rs, device, add):
        part = pl.ds(c * XSUB, XSUB)
        value = x_term(shift, c)
        if add:
            arrived(came.at[0, part], ss.at[0, c], rs.at[0, c])
            value = value + came[0, part, :].astype(F32)
        out[s, part, :] = value.astype(BF16)
        send(out.at[s, part], came.at[s, part], ss.at[s, c], rs.at[s, c], device)

    def x_down(s, c, shift, add=False):
        x_hop(s, c, shift, xd_out, xd_in, xd_ss, xd_rs, x_dn, add)

    def x_over(s, c, shift, add=False):
        x_hop(s, c, shift, xu_out, xu_in, xu_ss, xu_rs, x_up, add)

    def z_step(s):
        for c in range(NSUB):
            hop(s, c, 4 - s, up_out, up_in, up_ss, up_rs, z_up)
            if s < 3:
                hop(s, c, 5 + s, dn_out, dn_in, dn_ss, dn_rs, z_dn)

    z_step(0)

    x_down(0, 0, 2)
    x_over(0, 2, 2)
    x_down(0, 1, 2)
    x_over(0, 3, 2)
    for c in (2, 3):
        x_down(1, c, 3)
        x_over(1, c - 2, 1)

    for i in (1, 2, 3):
        arrived(texts.at[2 * i], text_ss.at[i], text_rs.at[i])
        send(
            texts.at[2 * i],
            texts.at[2 * i + 1 - 2 * core],
            text_ss.at[3 + i],
            text_rs.at[3 + i],
            (sibling, mp),
        )
        arrived(images.at[2 * i], img_ss.at[i], img_rs.at[i])
        send(
            images.at[2 * i],
            images.at[2 * i - 1 + 2 * core],
            img_ss.at[3 + i],
            img_rs.at[3 + i],
            (sibling, mp),
        )

    z_step(1)

    for c in (0, 1):
        x_down(1, c, 3, True)
        x_over(1, c + 2, 1, True)

    arrived(texts.at[7 - 6 * core], text_ss.at[0], text_rs.at[0])
    arrived(images.at[1 + 6 * core], img_ss.at[0], img_rs.at[0])
    for i in (1, 2, 3):
        arrived(texts.at[2 * i - 1 + 2 * core], text_ss.at[3 + i], text_rs.at[3 + i])
        arrived(images.at[2 * i + 1 - 2 * core], img_ss.at[3 + i], img_rs.at[3 + i])

    scale = scale_ref[0]
    bias = bias_ref[0]

    def slope_of(logits, positive):
        label = jnp.where(positive, 1.0, -1.0).astype(F32)
        return (-label * jax.nn.sigmoid(-label * logits)).astype(BF16)

    def target_of(marked):
        return marked[0:1, :] * float(TXTS) + marked[1:2, :]

    def project(value, unit, norm):
        return (value - unit * jnp.sum(unit * value, axis=-1, keepdims=True)) / norm

    words = own_texts[...]
    text_ids = lax.broadcasted_iota(jnp.int32, (TXTS, 128), 0).astype(F32)
    second = (lax.broadcasted_iota(jnp.int32, (TXTS, 128), 1) // IMGS).astype(F32)
    lane_second = lax.broadcasted_iota(jnp.int32, (16, 128), 1) >= IMGS
    dtxt = jnp.zeros((TXTS, D), F32)
    for pair in range(STEPS // 2):
        block = images[2 * pair : 2 * pair + 2, :, 0:D].reshape(2 * IMGS, D)
        logits = scale * nt_dot(words, block) + bias
        first = images[2 * pair, 0:16, D : D + META].astype(F32)
        later = images[2 * pair + 1, 0:16, D : D + META].astype(F32)
        target = target_of(jnp.where(lane_second, later, first))
        positive = target == (text_ids + (second + float(2 * pair)) * float(TXTS))
        dtxt = dtxt + nn_dot(slope_of(logits, positive), block)
    gt_out[...] = project(scale * dtxt, txt_unit[...], txt_norm[:, 0:1]).astype(BF16)
    send(gt_out, gt_in, pair_ss.at[2], pair_rs.at[2], (me, 1 - mp))

    z_step(2)

    arrived(img_too, pair_ss.at[3], pair_rs.at[3])
    full = img_too[:, 0:D].astype(F32)
    norm = jnp.sqrt(jnp.sum(full * full, axis=-1, keepdims=True) + EPS)
    unit = full / norm
    img_unit[IMGS:, :] = unit
    img_norm[IMGS:, :] = jnp.broadcast_to(norm, (IMGS, 128))
    both[0:IMGS, :] = images[0, :, 0:D]
    both[IMGS:, :] = unit.astype(BF16)

    def as_column(marked):
        line = target_of(marked.astype(F32))[:, 0:IMGS]
        return jnp.sum(jnp.where(mark_row == mark_col, line, 0.0), axis=-1, keepdims=True)

    want = jnp.concatenate(
        [as_column(img_in[0:16, D : D + META]), as_column(img_too[0:16, D : D + META])], axis=0
    )
    lane = lax.broadcasted_iota(jnp.int32, (2 * IMGS, 2 * HTXT), 1)
    pictures = both[...]
    dimg = jnp.zeros((2 * IMGS, D), F32)
    for pair in range(STEPS // 2):
        block = texts[2 * pair : 2 * pair + 2].reshape(2 * HTXT, D)
        starts = [k * TXTS + near(-k)[1] * HTXT for k in (2 * pair, 2 * pair + 1)]
        column = jnp.where(lane < HTXT, lane + starts[0], lane + (starts[1] - HTXT))
        logits = scale * nt_dot(pictures, block) + bias
        dimg = dimg + nn_dot(slope_of(logits, want == column.astype(F32)), block)
    dimg = project(scale * dimg, img_unit[...], img_norm[:, 0:1])
    gimg[...] = dimg[0:IMGS, :]
    gi_out[...] = dimg[IMGS:, :].astype(BF16)
    send(gi_out, gi_in, pair_ss.at[4], pair_rs.at[4], (me, 1 - mp))

    z_step(3)

    for c in range(NXSUB):
        part = pl.ds(c * XSUB, XSUB)
        arrived(xd_in.at[1, part], xd_ss.at[1, c], xd_rs.at[1, c])
        arrived(xu_in.at[1, part], xu_ss.at[1, c], xu_rs.at[1, c])
        value = x_term(0, c) + xd_in[1, part, :].astype(F32) + xu_in[1, part, :].astype(F32)
        xsum[part, :] = value
        xsum_bf[part, :] = value.astype(BF16)

    for q in (4, 3, 5, 2, 6, 1, 7):
        send(
            xsum_bf.at[rows((zpos + q) % NZ * ZWIN, ZWIN)],
            zwin_in.at[q - 1],
            zwin_ss.at[q - 1],
            zwin_rs.at[q - 1],
            along_z(q),
        )

    arrived(inner_in, inner_ss, inner_rs)

    @pl.loop(0, TOK // LN)
    def _(i):
        r = rows(i * LN, LN)
        total = inner_out[r, :].astype(F32) + inner_in[r, :].astype(F32)
        gacts[r, :] = (cot[r, :].astype(F32) + rstd[r, 0:1] * total).astype(BF16)

    base = zpos * ZROWS
    for c in range(NSUB):
        part = pl.ds(c * SUB, SUB)
        arrived(up_in.at[3, part], up_ss.at[3, c], up_rs.at[3, c])
        arrived(dn_in.at[2, part], dn_ss.at[2, c], dn_rs.at[2, c])
        value = (
            grads[rows(base + c * SUB, SUB), 0:CZ]
            + up_in[3, part, :].astype(F32)
            + dn_in[2, part, :].astype(F32)
        )
        zsum[part, :] = value
        zsum_bf[part, :] = value.astype(BF16)
    for q in (6, 5, 4, 3, 2, 7, 1):
        there = (plane + q) % 8
        send(
            zsum_bf.at[rows(there * 16, WIN)],
            win_in.at[q - 1],
            win_ss.at[q - 1],
            win_rs.at[q - 1],
            in_plane(q),
        )

    total = xsum[rows(zpos * ZWIN, ZWIN), :]
    for q in range(1, 8):
        arrived(zwin_in.at[q - 1], zwin_ss.at[q - 1], zwin_rs.at[q - 1])
        total = total + zwin_in[q - 1].astype(F32)

    def turned(value, start):
        size = value.shape[0]
        return pltpu.roll(value, (size - start) % size, 0)

    lower, upper = total[0:HWIN, :], total[HWIN:, :]
    y_out[...] = jnp.concatenate(
        [jnp.where(half == 0, upper, lower), jnp.zeros((WIN - HWIN, CX), F32)], axis=0
    ).astype(BF16)
    send(y_out, y_in, y_ss, y_rs, in_plane(4))
    mine_x = jnp.where(half == 0, lower, upper)

    arrived(gt_in, pair_ss.at[2], pair_rs.at[2])
    gtxt[...] = gt_out[...].astype(F32) + gt_in[...].astype(F32)
    arrived(gi_in, pair_ss.at[4], pair_rs.at[4])
    gimg[...] = gimg[...] + gi_in[...].astype(F32)

    total = zsum[rows(plane * 16, WIN), :]
    for q in range(1, 8):
        arrived(win_in.at[q - 1], win_ss.at[q - 1], win_rs.at[q - 1])
        total = total + win_in[q - 1].astype(F32)
    mine_z = turned(total, 2 * plane)
    arrived(y_in, y_ss, y_rs)
    mine_x = turned(mine_x + y_in[...].astype(F32)[0:HWIN, :], 2 * xpos)
    fin_out[:, 0:CZ] = turned(mine_z, OUT * (1 - core))[0:16, :]
    fin_out[:, CZ:] = turned(mine_x, OUT * (1 - core))[0:16, :]
    send(fin_out, fin_in, fin_ss, fin_rs, (sibling, mp))
    keep = jnp.concatenate(
        [turned(mine_z, OUT * core)[0:OUT, :], turned(mine_x, OUT * core)[0:OUT, :]], axis=1
    )
    arrived(fin_in, fin_ss, fin_rs)
    other = fin_in[0:OUT, :]
    gup[...] = jnp.where(core == 0, keep, other)
    gdn[...] = jnp.where(core == 0, other, keep)

    for copy in pending:
        copy.wait_send()


def hand_over(*refs):
    for i in range(5):
        refs[5 + i][...] = refs[i][...]


def shards(
    img_emb, txt_emb, logit_scale, logit_bias, pos_step, pos_row, acts, cotangent, w_up, w_down
):
    pstep = pos_step.reshape(1, IMGS)
    prow = pos_row.reshape(1, IMGS)
    vmem = pl.BlockSpec(memory_space=pltpu.VMEM)
    smem = pl.BlockSpec(memory_space=pltpu.SMEM)
    hbm = pl.BlockSpec(memory_space=pl.ANY)
    dma = pltpu.SemaphoreType.DMA
    out = pl.pallas_call(
        step_kernel,
        out_shape=(
            jax.ShapeDtypeStruct((IMGS, D), F32),
            jax.ShapeDtypeStruct((TXTS, D), F32),
            jax.ShapeDtypeStruct((OUT, HALF), F32),
            jax.ShapeDtypeStruct((OUT, HALF), F32),
            jax.ShapeDtypeStruct((TOK, D), BF16),
        ),
        in_specs=[smem, smem, hbm, hbm, vmem, vmem, hbm, hbm, hbm, hbm],
        out_specs=(vmem, vmem, vmem, vmem, vmem),
        scratch_shapes=[
            pltpu.VMEM((IMGS, D + META), BF16),
            pltpu.VMEM((TXTS, D), BF16),
            pltpu.VMEM((TOK, D), BF16),
            pltpu.VMEM((TOK, D), BF16),
            pltpu.VMEM((D, HALF), BF16),
            pltpu.VMEM((D, HALF), BF16),
            pltpu.VMEM((2, TOK, D), BF16),
            pltpu.VMEM((2, TOK, HALF), BF16),
            pltpu.VMEM((TOK, D), BF16),
            pltpu.VMEM((TOK, HALF), BF16),
            pltpu.VMEM((TOK, D), F32),
            pltpu.VMEM((TOK, 128), F32),
            pltpu.VMEM((TOK, D), F32),
            pltpu.VMEM((D, HALF), F32),
            pltpu.VMEM((4, ZROWS, CZ), BF16),
            pltpu.VMEM((4, ZROWS, CZ), BF16),
            pltpu.VMEM((3, ZROWS, CZ), BF16),
            pltpu.VMEM((3, ZROWS, CZ), BF16),
            pltpu.VMEM((TOK, D), BF16),
            pltpu.VMEM((TOK, D), BF16),
            pltpu.VMEM((2, XROWS, CX), BF16),
            pltpu.VMEM((2, XROWS, CX), BF16),
            pltpu.VMEM((2, XROWS, CX), BF16),
            pltpu.VMEM((2, XROWS, CX), BF16),
            pltpu.VMEM((ZROWS, CZ), F32),
            pltpu.VMEM((ZROWS, CZ), BF16),
            pltpu.VMEM((XROWS, CX), F32),
            pltpu.VMEM((XROWS, CX), BF16),
            pltpu.VMEM((7, WIN, CZ), BF16),
            pltpu.VMEM((7, ZWIN, CX), BF16),
            pltpu.VMEM((WIN, CX), BF16),
            pltpu.VMEM((WIN, CX), BF16),
            pltpu.VMEM((16, HALF), F32),
            pltpu.VMEM((16, HALF), F32),
            pltpu.VMEM((TXTS, D), BF16),
            pltpu.VMEM((STEPS, HTXT, D), BF16),
            pltpu.VMEM((STEPS, IMGS, D + META), BF16),
            pltpu.VMEM((IMGS, D + META), BF16),
            pltpu.VMEM((2 * IMGS, D), BF16),
            pltpu.VMEM((TXTS, D), F32),
            pltpu.VMEM((TXTS, 128), F32),
            pltpu.VMEM((2 * IMGS, D), F32),
            pltpu.VMEM((2 * IMGS, 128), F32),
            pltpu.VMEM((TXTS, D), BF16),
            pltpu.VMEM((TXTS, D), BF16),
            pltpu.VMEM((IMGS, D), BF16),
            pltpu.VMEM((IMGS, D), BF16),
            dma((6,)),
            dma((7,)),
            dma((7,)),
            dma((7,)),
            dma((7,)),
            dma((5,)),
            dma((5,)),
            dma((4, NSUB)),
            dma((4, NSUB)),
            dma((3, NSUB)),
            dma((3, NSUB)),
            dma,
            dma,
            dma((2, NXSUB)),
            dma((2, NXSUB)),
            dma((2, NXSUB)),
            dma((2, NXSUB)),
            dma((7,)),
            dma((7,)),
            dma((7,)),
            dma((7,)),
            dma,
            dma,
            dma,
            dma,
        ],
        compiler_params=pltpu.CompilerParams(
            collective_id=0, has_side_effects=True, vmem_limit_bytes=58 * 1024 * 1024
        ),
        name="step",
    )(logit_scale, logit_bias, img_emb, txt_emb, pstep, prow, acts, cotangent, w_up, w_down)
    return pl.pallas_call(
        hand_over,
        out_shape=tuple(jax.ShapeDtypeStruct(x.shape, x.dtype) for x in out),
        in_specs=[vmem] * 5,
        out_specs=(vmem,) * 5,
        name="hand_over",
    )(*out)


def solution(mesh):
    return jax.shard_map(
        shards,
        mesh=mesh,
        in_specs=(
            P(("dp", "mp"), None),
            P("dp", None),
            P(),
            P(),
            P(("dp", "mp")),
            P(("dp", "mp")),
            P("dp", None),
            P("dp", None),
            P(None, "mp"),
            P(None, "mp"),
        ),
        out_specs=(
            P(("dp", "mp"), None),
            P("dp", None),
            P("dp", "mp"),
            P("dp", "mp"),
            P("dp", None),
        ),
        check_vma=False,
    )
```

```python
import jax
import jax.numpy as jnp
from jax import lax
from jax.experimental import pallas as pl
from jax.experimental.pallas import tpu as pltpu
from jax.sharding import PartitionSpec as P

D = 1152
STEPS = 8
IMGS = 64
TXTS = 128
HTXT = 64
TOK = 384
HALF = 1152
NZ = 8
ZROWS = D // NZ
SUB = 48
NSUB = ZROWS // SUB
CZ = 768
CX = HALF - CZ
NX = 4
HWIN = 24
ZWIN = 2 * HWIN
XROWS = NZ * ZWIN
XSUB = 2 * ZWIN
NXSUB = XROWS // XSUB
OUT = 9
META = 128
LN = 64
EPS = 1e-06
MESH = pl.DeviceIdType.MESH
F32 = jnp.float32
BF16 = jnp.bfloat16
GELU_C = 0.7978845608028654
GELU_A = 0.044715
TILES = ((0, 256), (256, 256), (512, 256), (768, 256), (1024, 128))


def rows(start, size, align=16):
    return pl.ds(pl.multiple_of(start, align), size)


def nt_dot(a, b):
    return lax.dot_general(a, b, (((1,), (1,)), ((), ())), preferred_element_type=F32)


def tn_dot(a, b):
    return lax.dot_general(a, b, (((0,), (0,)), ((), ())), preferred_element_type=F32)


def nn_dot(a, b):
    return jnp.dot(a, b, preferred_element_type=F32)


def wide_tiles(body):
    @pl.loop(0, 4)
    def _(t):
        body(pl.multiple_of(t * 256, 256), 256)

    body(1024, 128)


def step_kernel(
    scale_ref,
    bias_ref,
    img_h,
    txt_h,
    pstep,
    prow,
    acts_h,
    cot_h,
    wup_h,
    wdn_h,
    gimg_h,
    gtxt_h,
    gup_h,
    gdn_h,
    gacts_h,
    gimg,
    gtxt,
    gup,
    gdn,
    gacts,
    img_in,
    txt_in,
    acts,
    cot,
    wup,
    wdn,
    pair_l,
    pair_r,
    left_in,
    right_in,
    normed,
    rstd,
    dnorm,
    grads,
    up_out,
    up_in,
    dn_out,
    dn_in,
    inner_out,
    inner_in,
    xd_out,
    xd_in,
    xu_out,
    xu_in,
    zsum,
    xsum,
    xsum_bf,
    win_out,
    win_in,
    zwin_in,
    y_out,
    y_in,
    parts,
    own_texts,
    texts,
    images,
    img_too,
    both,
    txt_unit,
    txt_norm,
    img_unit,
    img_norm,
    gt_out,
    gt_in,
    gi_out,
    gi_in,
    in_sem,
    text_ss,
    text_rs,
    img_ss,
    img_rs,
    pair_ss,
    pair_rs,
    up_ss,
    up_rs,
    dn_ss,
    dn_rs,
    inner_ss,
    inner_rs,
    xd_ss,
    xd_rs,
    xu_ss,
    xu_rs,
    win_ss,
    win_rs,
    zwin_ss,
    zwin_rs,
    y_ss,
    y_rs,
):
    me = lax.axis_index("dp")
    mp = lax.axis_index("mp")
    core = me % 2
    spot = me % 8
    plane = (me // 2) % 8
    zpos = me // 16
    sibling = me + 1 - 2 * core

    def near(shift):
        moved = spot + shift
        crossed = (moved + 8) // 8
        return ((me + shift + 128) % 128, (mp + crossed + 1) % 2)

    def in_plane(turn, to_core):
        return ((zpos * 8 + (plane + turn) % 8) * 2 + to_core, mp)

    special = ((me + 7 * (2 * core - 1) + 128) % 128, (mp + 1) % 2)
    xpos = plane % 4
    half = plane // 4
    x_up = (me + 2 * ((xpos + 1) % 4 - xpos), mp)
    x_dn = (me + 2 * ((xpos + 3) % 4 - xpos), mp)

    def along_z(turn):
        return ((me + 16 * turn) % 128, mp)

    z_up = along_z(1)
    z_dn = along_z(7)

    def load(source, target, i):
        copy = pltpu.make_async_copy(source, target, in_sem.at[i])
        copy.start()
        return copy

    acts_load = load(acts_h, acts, 0)
    txt_load = load(txt_h, txt_in, 1)
    img_load = load(img_h, img_in.at[:, pl.ds(0, D)], 2)
    wup_load = load(wup_h, wup, 3)
    cot_load = load(cot_h, cot, 4)
    wdn_load = load(wdn_h, wdn, 5)

    barrier = pltpu.get_barrier_semaphore()
    partners = [near(s) for s in (2, 4, 6, -2, -4, -6)]
    partners += [(sibling, mp), special, (me, 1 - mp)]
    partners += [along_z(q) for q in range(1, 8)]
    partners += [in_plane(q, to) for q in range(1, 8) for to in (core, 1 - core)]
    for partner in partners:
        pl.semaphore_signal(barrier, inc=1, device_id=partner, device_id_type=MESH)

    def send(source, target, send_sem, recv_sem, device):
        copy = pltpu.make_async_remote_copy(
            src_ref=source,
            dst_ref=target,
            send_sem=send_sem,
            recv_sem=recv_sem,
            device_id=device,
            device_id_type=MESH,
        )
        copy.start()
        pending.append(copy)

    def arrived(target, send_sem, recv_sem):
        pltpu.make_async_remote_copy(
            src_ref=target,
            dst_ref=target,
            send_sem=send_sem,
            recv_sem=recv_sem,
            device_id=(sibling, mp),
            device_id_type=MESH,
        ).wait_recv()

    pending = []

    txt_load.wait()

    @pl.loop(0, TXTS // LN)
    def _(i):
        r = rows(i * LN, LN)
        full = txt_in[r, :].astype(F32)
        norm = jnp.sqrt(jnp.sum(full * full, axis=-1, keepdims=True) + EPS)
        unit = full / norm
        txt_unit[r, :] = unit
        txt_norm[r, :] = jnp.broadcast_to(norm, (LN, 128))
        own_texts[r, :] = unit.astype(BF16)

    img_load.wait()

    @pl.loop(0, IMGS // LN)
    def _(i):
        r = rows(i * LN, LN)
        full = img_in[r, 0:D].astype(F32)
        norm = jnp.sqrt(jnp.sum(full * full, axis=-1, keepdims=True) + EPS)
        unit = full / norm
        img_unit[r, :] = unit
        img_norm[r, :] = jnp.broadcast_to(norm, (LN, 128))
        images[0, r, 0:D] = unit.astype(BF16)

    texts[0] = own_texts[rows(mp * HTXT, HTXT), :]

    mark_row = lax.broadcasted_iota(jnp.int32, (IMGS, IMGS), 0)
    mark_col = lax.broadcasted_iota(jnp.int32, (IMGS, IMGS), 1)
    marks = jnp.where(mark_row == 0, pstep[...], prow[...]).astype(F32).astype(BF16)
    for place in (0, IMGS):
        images[0, :, D + place : D + place + IMGS] = marks
        img_in[:, D + place : D + place + IMGS] = marks

    acts_load.wait()

    @pl.loop(0, TOK // LN)
    def _(i):
        r = rows(i * LN, LN)
        full = acts[r, :].astype(F32)
        mean = jnp.mean(full, axis=-1, keepdims=True)
        centred = full - mean
        scale = lax.rsqrt(jnp.mean(centred * centred, axis=-1, keepdims=True) + EPS)
        out = centred * scale
        normed[r, :] = out
        rstd[r, :] = jnp.broadcast_to(scale, (LN, 128))
        pair_l[core, r, :] = out.astype(BF16)

    cot_load.wait()

    @pl.loop(0, TOK // LN)
    def _(i):
        r = rows(i * LN, LN)
        pair_l[1 - core, r, :] = cot[r, :]

    pl.semaphore_wait(barrier, len(partners))

    send(pair_l.at[1], left_in, pair_ss.at[0], pair_rs.at[0], (sibling, mp))

    send(img_in, img_too, pair_ss.at[3], pair_rs.at[3], (me, 1 - mp))
    for i in (1, 3):
        send(texts.at[0], texts.at[2 * i], text_ss.at[i], text_rs.at[i], near(2 * i))
        send(images.at[0], images.at[2 * i], img_ss.at[i], img_rs.at[i], near(-2 * i))
    text_special = (
        (1 - core) * sibling + core * special[0],
        (1 - core) * mp + core * special[1],
    )
    img_special = (
        core * sibling + (1 - core) * special[0],
        core * mp + (1 - core) * special[1],
    )
    send(texts.at[0], texts.at[1 + 6 * core], text_ss.at[0], text_rs.at[0], text_special)
    send(images.at[0], images.at[7 - 6 * core], img_ss.at[0], img_rs.at[0], img_special)

    wup_load.wait()
    wdn_load.wait()

    def hidden_tile(start, width):
        c = pl.ds(start, width)
        pre = nn_dot(pair_l[core, :, :], wup[:, c])
        dhidden = nn_dot(cot[...], wdn[:, c])
        square = pre * pre
        t = jnp.tanh(GELU_C * (pre + GELU_A * (square * pre)))
        half = 0.5 * (1.0 + t)
        slope = half + (0.5 * GELU_C) * pre * (1.0 - t * t) * (1.0 + (3.0 * GELU_A) * square)
        pair_r[1 - core, :, c] = (pre * half).astype(BF16)
        pair_r[core, :, c] = (dhidden * slope).astype(BF16)

    wide_tiles(hidden_tile)
    send(pair_r.at[1], right_in, pair_ss.at[1], pair_rs.at[1], (sibling, mp))

    def dnorm_tile(start, width):
        c = pl.ds(start, width)
        dnorm[:, c] = nt_dot(pair_r[core, :, :], wup[c, :])

    wide_tiles(dnorm_tile)

    @pl.loop(0, TOK // LN)
    def _(i):
        r = rows(i * LN, LN)
        value = dnorm[r, :]
        unit = normed[r, :]
        inner = (
            value
            - jnp.mean(value, axis=-1, keepdims=True)
            - unit * jnp.mean(value * unit, axis=-1, keepdims=True)
        )
        inner_out[r, :] = inner.astype(BF16)

    send(inner_out, inner_in, inner_ss, inner_rs, (me, 1 - mp))

    def hand_on(i):
        send(
            texts.at[2 * i],
            texts.at[2 * i + 1 - 2 * core],
            text_ss.at[3 + i],
            text_rs.at[3 + i],
            (sibling, mp),
        )
        send(
            images.at[2 * i],
            images.at[2 * i - 1 + 2 * core],
            img_ss.at[3 + i],
            img_rs.at[3 + i],
            (sibling, mp),
        )

    arrived(texts.at[2], text_ss.at[1], text_rs.at[1])
    send(texts.at[2], texts.at[4], text_ss.at[2], text_rs.at[2], near(2))
    arrived(images.at[2], img_ss.at[1], img_rs.at[1])
    send(images.at[2], images.at[4], img_ss.at[2], img_rs.at[2], near(-2))
    hand_on(1)

    arrived(left_in, pair_ss.at[0], pair_rs.at[0])
    arrived(right_in, pair_ss.at[1], pair_rs.at[1])

    def grad_tile(start, width):
        c = pl.ds(start, width)
        grads[c, :] = tn_dot(pair_l[0, :, c], pair_r[0]) + tn_dot(left_in[:, c], right_in[...])

    wide_tiles(grad_tile)

    def hop(s, c, shift, out, came, ss, rs, device):
        base = ((zpos + shift) % NZ) * ZROWS
        part = pl.ds(c * SUB, SUB)
        value = grads[rows(base + c * SUB, SUB), 0:CZ]
        if s > 0:
            arrived(came.at[s - 1, part], ss.at[s - 1, c], rs.at[s - 1, c])
            value = value + came[s - 1, part, :].astype(F32)
        out[s, part, :] = value.astype(BF16)
        send(out.at[s, part], came.at[s, part], ss.at[s, c], rs.at[s, c], device)

    def x_term(shift, c):
        there = (xpos + shift) % NX
        return jnp.concatenate(
            [
                grads[rows(144 * z + 72 * h + 16 * there, HWIN, 8), CZ:]
                for z in (2 * c, 2 * c + 1)
                for h in (0, 1)
            ],
            axis=0,
        )

    def x_hop(s, c, shift, out, came, ss, rs, device, add):
        part = pl.ds(c * XSUB, XSUB)
        value = x_term(shift, c)
        if add:
            arrived(came.at[0, part], ss.at[0, c], rs.at[0, c])
            value = value + came[0, part, :].astype(F32)
        out[s, part, :] = value.astype(BF16)
        send(out.at[s, part], came.at[s, part], ss.at[s, c], rs.at[s, c], device)

    def x_down(s, c, shift, add=False):
        x_hop(s, c, shift, xd_out, xd_in, xd_ss, xd_rs, x_dn, add)

    def x_over(s, c, shift, add=False):
        x_hop(s, c, shift, xu_out, xu_in, xu_ss, xu_rs, x_up, add)

    def z_step(s):
        for c in range(NSUB):
            hop(s, c, 4 - s, up_out, up_in, up_ss, up_rs, z_up)
            if s < 3:
                hop(s, c, 5 + s, dn_out, dn_in, dn_ss, dn_rs, z_dn)

    z_step(0)

    x_down(0, 0, 2)
    x_over(0, 2, 2)
    x_down(0, 1, 2)
    x_over(0, 3, 2)
    for c in (2, 3):
        x_down(1, c, 3)
        x_over(1, c - 2, 1)

    z_step(1)

    for c in (0, 1):
        x_down(1, c, 3, True)
        x_over(1, c + 2, 1, True)

    for i in (3, 2):
        arrived(texts.at[2 * i], text_ss.at[i], text_rs.at[i])
        arrived(images.at[2 * i], img_ss.at[i], img_rs.at[i])
        hand_on(i)

    z_step(2)

    arrived(texts.at[7 - 6 * core], text_ss.at[0], text_rs.at[0])
    arrived(images.at[1 + 6 * core], img_ss.at[0], img_rs.at[0])
    for i in (1, 2, 3):
        arrived(texts.at[2 * i - 1 + 2 * core], text_ss.at[3 + i], text_rs.at[3 + i])
        arrived(images.at[2 * i + 1 - 2 * core], img_ss.at[3 + i], img_rs.at[3 + i])

    scale = scale_ref[0]
    bias = bias_ref[0]

    def slope_of(logits, positive):
        label = jnp.where(positive, 1.0, -1.0).astype(F32)
        return (-label * jax.nn.sigmoid(-label * logits)).astype(BF16)

    def target_of(marked):
        return marked[0:1, :] * float(TXTS) + marked[1:2, :]

    def project(value, unit, norm):
        return (value - unit * jnp.sum(unit * value, axis=-1, keepdims=True)) / norm

    words = own_texts[...]
    text_ids = lax.broadcasted_iota(jnp.int32, (TXTS, 128), 0).astype(F32)
    second = (lax.broadcasted_iota(jnp.int32, (TXTS, 128), 1) // IMGS).astype(F32)
    lane_second = lax.broadcasted_iota(jnp.int32, (16, 128), 1) >= IMGS
    dtxt = jnp.zeros((TXTS, D), F32)
    for pair in range(STEPS // 2):
        block = images[2 * pair : 2 * pair + 2, :, 0:D].reshape(2 * IMGS, D)
        logits = scale * nt_dot(words, block) + bias
        first = images[2 * pair, 0:16, D : D + META].astype(F32)
        later = images[2 * pair + 1, 0:16, D : D + META].astype(F32)
        target = target_of(jnp.where(lane_second, later, first))
        positive = target == (text_ids + (second + float(2 * pair)) * float(TXTS))
        dtxt = dtxt + nn_dot(slope_of(logits, positive), block)
    gt_out[...] = project(scale * dtxt, txt_unit[...], txt_norm[:, 0:1]).astype(BF16)
    send(gt_out, gt_in, pair_ss.at[2], pair_rs.at[2], (me, 1 - mp))

    z_step(3)

    for c in range(NXSUB):
        part = pl.ds(c * XSUB, XSUB)
        arrived(xd_in.at[1, part], xd_ss.at[1, c], xd_rs.at[1, c])
        arrived(xu_in.at[1, part], xu_ss.at[1, c], xu_rs.at[1, c])
        value = x_term(0, c) + xd_in[1, part, :].astype(F32) + xu_in[1, part, :].astype(F32)
        xsum[part, :] = value
        xsum_bf[part, :] = value.astype(BF16)

    for q in (4, 3, 5, 2, 6, 1, 7):
        send(
            xsum_bf.at[rows((zpos + q) % NZ * ZWIN, ZWIN)],
            zwin_in.at[q - 1],
            zwin_ss.at[q - 1],
            zwin_rs.at[q - 1],
            along_z(q),
        )

    arrived(img_too, pair_ss.at[3], pair_rs.at[3])
    full = img_too[:, 0:D].astype(F32)
    norm = jnp.sqrt(jnp.sum(full * full, axis=-1, keepdims=True) + EPS)
    unit = full / norm
    img_unit[IMGS:, :] = unit
    img_norm[IMGS:, :] = jnp.broadcast_to(norm, (IMGS, 128))
    both[0:IMGS, :] = images[0, :, 0:D]
    both[IMGS:, :] = unit.astype(BF16)

    def as_column(marked):
        line = target_of(marked.astype(F32))[:, 0:IMGS]
        return jnp.sum(jnp.where(mark_row == mark_col, line, 0.0), axis=-1, keepdims=True)

    want = jnp.concatenate(
        [as_column(img_in[0:16, D : D + META]), as_column(img_too[0:16, D : D + META])], axis=0
    )
    lane = lax.broadcasted_iota(jnp.int32, (2 * IMGS, 2 * HTXT), 1)
    pictures = both[...]
    dimg = jnp.zeros((2 * IMGS, D), F32)
    for pair in range(STEPS // 2):
        block = texts[2 * pair : 2 * pair + 2].reshape(2 * HTXT, D)
        starts = [k * TXTS + near(-k)[1] * HTXT for k in (2 * pair, 2 * pair + 1)]
        column = jnp.where(lane < HTXT, lane + starts[0], lane + (starts[1] - HTXT))
        logits = scale * nt_dot(pictures, block) + bias
        dimg = dimg + nn_dot(slope_of(logits, want == column.astype(F32)), block)
    dimg = project(scale * dimg, img_unit[...], img_norm[:, 0:1])
    gimg[...] = dimg[0:IMGS, :]
    gi_out[...] = dimg[IMGS:, :].astype(BF16)
    send(gi_out, gi_in, pair_ss.at[4], pair_rs.at[4], (me, 1 - mp))

    arrived(inner_in, inner_ss, inner_rs)

    @pl.loop(0, TOK // LN)
    def _(i):
        r = rows(i * LN, LN)
        total = inner_out[r, :].astype(F32) + inner_in[r, :].astype(F32)
        gacts[r, :] = (cot[r, :].astype(F32) + rstd[r, 0:1] * total).astype(BF16)

    stores = [load(gacts, gacts_h, 6)]

    base = zpos * ZROWS
    for c in range(NSUB):
        part = pl.ds(c * SUB, SUB)
        arrived(up_in.at[3, part], up_ss.at[3, c], up_rs.at[3, c])
        arrived(dn_in.at[2, part], dn_ss.at[2, c], dn_rs.at[2, c])
        value = (
            grads[rows(base + c * SUB, SUB), 0:CZ]
            + up_in[3, part, :].astype(F32)
            + dn_in[2, part, :].astype(F32)
        )
        zsum[part, :] = value
    zsum[ZROWS:, :] = jnp.zeros((16, CZ), F32)
    for there in range(8):
        for to in range(2):
            first = 2 * OUT * there + OUT * to
            win_out[there, to] = zsum[first : first + 16, :].astype(BF16)
    for q in (6, 2, 5, 3, 4, 7, 1, 0):
        for to in (core, 1 - core)[q == 0 :]:
            send(
                win_out.at[(plane + q) % 8, to],
                win_in.at[core, q],
                win_ss.at[to, q],
                win_rs.at[core, q],
                in_plane(q, to),
            )
    win_in[core, 0] = win_out[plane, core]

    total = xsum[rows(zpos * ZWIN, ZWIN), :]
    for q in range(1, 8):
        arrived(zwin_in.at[q - 1], zwin_ss.at[q - 1], zwin_rs.at[q - 1])
        total = total + zwin_in[q - 1].astype(F32)

    parts[0:ZWIN, :] = pltpu.roll(total, (ZWIN - 2 * xpos) % ZWIN, 0)
    parts[ZWIN:, :] = jnp.zeros((16, CX), F32)
    for to_half in range(2):
        for to in range(2):
            first = HWIN * to_half + OUT * to
            y_out[to_half, to] = parts[first : first + 16, :].astype(BF16)
    for other, to in ((1, core), (1, 1 - core), (0, 1 - core)):
        send(
            y_out.at[(half + other) % 2, to],
            y_in.at[core, other],
            y_ss.at[to, other],
            y_rs.at[core, other],
            in_plane(4 * other, to),
        )
    y_in[core, 0] = y_out[half, core]

    arrived(gt_in, pair_ss.at[2], pair_rs.at[2])
    gtxt[...] = gt_out[...].astype(F32) + gt_in[...].astype(F32)
    arrived(gi_in, pair_ss.at[4], pair_rs.at[4])
    gimg[...] = gimg[...] + gi_in[...].astype(F32)
    stores.append(load(gtxt, gtxt_h, 7))
    stores.append(load(gimg, gimg_h, 8))

    arrived(win_in.at[1 - core, 0], win_ss.at[1 - core, 0], win_rs.at[1 - core, 0])
    arrived(y_in.at[1 - core, 0], y_ss.at[1 - core, 0], y_rs.at[1 - core, 0])
    for origin, result in ((0, gup), (1, gdn)):
        total = win_in[origin, 0].astype(F32)
        for q in range(1, 8):
            arrived(win_in.at[origin, q], win_ss.at[origin, q], win_rs.at[origin, q])
            total = total + win_in[origin, q].astype(F32)
        result[:, 0:CZ] = total[0:OUT, :]
    for origin, result in ((0, gup), (1, gdn)):
        arrived(y_in.at[origin, 1], y_ss.at[origin, 1], y_rs.at[origin, 1])
        total = y_in[origin, 0].astype(F32) + y_in[origin, 1].astype(F32)
        result[:, CZ:] = total[0:OUT, :]
    stores.append(load(gup, gup_h, 9))
    stores.append(load(gdn, gdn_h, 10))
    for store in stores:
        store.wait()

    for copy in pending:
        copy.wait_send()


def hand_over(*refs):
    for i in range(5):
        refs[5 + i][...] = refs[i][...]


def shards(
    img_emb, txt_emb, logit_scale, logit_bias, pos_step, pos_row, acts, cotangent, w_up, w_down
):
    pstep = pos_step.reshape(1, IMGS)
    prow = pos_row.reshape(1, IMGS)
    vmem = pl.BlockSpec(memory_space=pltpu.VMEM)
    smem = pl.BlockSpec(memory_space=pltpu.SMEM)
    hbm = pl.BlockSpec(memory_space=pl.ANY)
    dma = pltpu.SemaphoreType.DMA
    out = pl.pallas_call(
        step_kernel,
        out_shape=(
            jax.ShapeDtypeStruct((IMGS, D), F32),
            jax.ShapeDtypeStruct((TXTS, D), F32),
            jax.ShapeDtypeStruct((OUT, HALF), F32),
            jax.ShapeDtypeStruct((OUT, HALF), F32),
            jax.ShapeDtypeStruct((TOK, D), BF16),
        ),
        in_specs=[smem, smem, hbm, hbm, vmem, vmem, hbm, hbm, hbm, hbm],
        out_specs=(hbm, hbm, hbm, hbm, hbm),
        scratch_shapes=[
            pltpu.VMEM((IMGS, D), F32),
            pltpu.VMEM((TXTS, D), F32),
            pltpu.VMEM((OUT, HALF), F32),
            pltpu.VMEM((OUT, HALF), F32),
            pltpu.VMEM((TOK, D), BF16),
            pltpu.VMEM((IMGS, D + META), BF16),
            pltpu.VMEM((TXTS, D), BF16),
            pltpu.VMEM((TOK, D), BF16),
            pltpu.VMEM((TOK, D), BF16),
            pltpu.VMEM((D, HALF), BF16),
            pltpu.VMEM((D, HALF), BF16),
            pltpu.VMEM((2, TOK, D), BF16),
            pltpu.VMEM((2, TOK, HALF), BF16),
            pltpu.VMEM((TOK, D), BF16),
            pltpu.VMEM((TOK, HALF), BF16),
            pltpu.VMEM((TOK, D), F32),
            pltpu.VMEM((TOK, 128), F32),
            pltpu.VMEM((TOK, D), F32),
            pltpu.VMEM((D, HALF), F32),
            pltpu.VMEM((4, ZROWS, CZ), BF16),
            pltpu.VMEM((4, ZROWS, CZ), BF16),
            pltpu.VMEM((3, ZROWS, CZ), BF16),
            pltpu.VMEM((3, ZROWS, CZ), BF16),
            pltpu.VMEM((TOK, D), BF16),
            pltpu.VMEM((TOK, D), BF16),
            pltpu.VMEM((2, XROWS, CX), BF16),
            pltpu.VMEM((2, XROWS, CX), BF16),
            pltpu.VMEM((2, XROWS, CX), BF16),
            pltpu.VMEM((2, XROWS, CX), BF16),
            pltpu.VMEM((ZROWS + 16, CZ), F32),
            pltpu.VMEM((XROWS, CX), F32),
            pltpu.VMEM((XROWS, CX), BF16),
            pltpu.VMEM((8, 2, 16, CZ), BF16),
            pltpu.VMEM((2, 8, 16, CZ), BF16),
            pltpu.VMEM((7, ZWIN, CX), BF16),
            pltpu.VMEM((2, 2, 16, CX), BF16),
            pltpu.VMEM((2, 2, 16, CX), BF16),
            pltpu.VMEM((ZWIN + 16, CX), F32),
            pltpu.VMEM((TXTS, D), BF16),
            pltpu.VMEM((STEPS, HTXT, D), BF16),
            pltpu.VMEM((STEPS, IMGS, D + META), BF16),
            pltpu.VMEM((IMGS, D + META), BF16),
            pltpu.VMEM((2 * IMGS, D), BF16),
            pltpu.VMEM((TXTS, D), F32),
            pltpu.VMEM((TXTS, 128), F32),
            pltpu.VMEM((2 * IMGS, D), F32),
            pltpu.VMEM((2 * IMGS, 128), F32),
            pltpu.VMEM((TXTS, D), BF16),
            pltpu.VMEM((TXTS, D), BF16),
            pltpu.VMEM((IMGS, D), BF16),
            pltpu.VMEM((IMGS, D), BF16),
            dma((11,)),
            dma((7,)),
            dma((7,)),
            dma((7,)),
            dma((7,)),
            dma((5,)),
            dma((5,)),
            dma((4, NSUB)),
            dma((4, NSUB)),
            dma((3, NSUB)),
            dma((3, NSUB)),
            dma,
            dma,
            dma((2, NXSUB)),
            dma((2, NXSUB)),
            dma((2, NXSUB)),
            dma((2, NXSUB)),
            dma((2, 8)),
            dma((2, 8)),
            dma((7,)),
            dma((7,)),
            dma((2, 2)),
            dma((2, 2)),
        ],
        compiler_params=pltpu.CompilerParams(
            collective_id=0, has_side_effects=True, vmem_limit_bytes=58 * 1024 * 1024
        ),
        name="step",
    )(logit_scale, logit_bias, img_emb, txt_emb, pstep, prow, acts, cotangent, w_up, w_down)
    return pl.pallas_call(
        hand_over,
        out_shape=tuple(jax.ShapeDtypeStruct(x.shape, x.dtype) for x in out),
        in_specs=[vmem] * 5,
        out_specs=(vmem,) * 5,
        name="hand_over",
    )(*out)


def solution(mesh):
    return jax.shard_map(
        shards,
        mesh=mesh,
        in_specs=(
            P(("dp", "mp"), None),
            P("dp", None),
            P(),
            P(),
            P(("dp", "mp")),
            P(("dp", "mp")),
            P("dp", None),
            P("dp", None),
            P(None, "mp"),
            P(None, "mp"),
        ),
        out_specs=(
            P(("dp", "mp"), None),
            P("dp", None),
            P("dp", "mp"),
            P("dp", "mp"),
            P("dp", None),
        ),
        check_vma=False,
    )
```

```python
import jax
import jax.numpy as jnp
from jax import lax
from jax.experimental import pallas as pl
from jax.experimental.pallas import tpu as pltpu
from jax.sharding import PartitionSpec as P

D = 1152
STEPS = 8
IMGS = 64
TXTS = 128
HTXT = 64
TOK = 384
HALF = 1152
NZ = 8
ZROWS = D // NZ
SUB = 48
NSUB = ZROWS // SUB
CZ = 768
CX = HALF - CZ
NX = 4
HWIN = 24
ZWIN = 2 * HWIN
XROWS = NZ * ZWIN
XSUB = 2 * ZWIN
NXSUB = XROWS // XSUB
OUT = 9
META = 128
LN = 64
EPS = 1e-06
MESH = pl.DeviceIdType.MESH
F32 = jnp.float32
BF16 = jnp.bfloat16
GELU_C = 0.7978845608028654
GELU_A = 0.044715
TILES = ((0, 256), (256, 256), (512, 256), (768, 256), (1024, 128))


def rows(start, size, align=16):
    return pl.ds(pl.multiple_of(start, align), size)


def nt_dot(a, b):
    return lax.dot_general(a, b, (((1,), (1,)), ((), ())), preferred_element_type=F32)


def tn_dot(a, b):
    return lax.dot_general(a, b, (((0,), (0,)), ((), ())), preferred_element_type=F32)


def nn_dot(a, b):
    return jnp.dot(a, b, preferred_element_type=F32)


def wide_tiles(body):
    @pl.loop(0, 4)
    def _(t):
        body(pl.multiple_of(t * 256, 256), 256)

    body(1024, 128)


def step_kernel(
    scale_ref,
    bias_ref,
    img_h,
    txt_h,
    pstep,
    prow,
    acts_h,
    cot_h,
    wup_h,
    wdn_h,
    gimg_h,
    gtxt_h,
    gup_h,
    gdn_h,
    gacts_h,
    gimg,
    gtxt,
    gup,
    gdn,
    gacts,
    img_in,
    txt_in,
    acts,
    cot,
    wup,
    wdn,
    pair_l,
    pair_r,
    left_in,
    right_in,
    normed,
    rstd,
    dnorm,
    grads,
    up_out,
    up_in,
    dn_out,
    dn_in,
    inner_out,
    inner_in,
    xd_out,
    xd_in,
    xu_out,
    xu_in,
    zsum,
    xsum,
    xsum_bf,
    win_out,
    win_in,
    zwin_in,
    y_out,
    y_in,
    parts,
    own_texts,
    texts,
    images,
    img_too,
    both,
    txt_unit,
    txt_norm,
    img_unit,
    img_norm,
    gt_out,
    gt_in,
    gi_out,
    gi_in,
    in_sem,
    text_ss,
    text_rs,
    img_ss,
    img_rs,
    pair_ss,
    pair_rs,
    up_ss,
    up_rs,
    dn_ss,
    dn_rs,
    inner_ss,
    inner_rs,
    xd_ss,
    xd_rs,
    xu_ss,
    xu_rs,
    win_ss,
    win_rs,
    zwin_ss,
    zwin_rs,
    y_ss,
    y_rs,
):
    me = lax.axis_index("dp")
    mp = lax.axis_index("mp")
    core = me % 2
    spot = me % 8
    plane = (me // 2) % 8
    zpos = me // 16
    sibling = me + 1 - 2 * core

    def near(shift):
        moved = spot + shift
        crossed = (moved + 8) // 8
        return ((me + shift + 128) % 128, (mp + crossed + 1) % 2)

    def in_plane(turn, to_core):
        return ((zpos * 8 + (plane + turn) % 8) * 2 + to_core, mp)

    special = ((me + 7 * (2 * core - 1) + 128) % 128, (mp + 1) % 2)
    xpos = plane % 4
    half = plane // 4
    x_up = (me + 2 * ((xpos + 1) % 4 - xpos), mp)
    x_dn = (me + 2 * ((xpos + 3) % 4 - xpos), mp)

    def along_z(turn):
        return ((me + 16 * turn) % 128, mp)

    z_up = along_z(1)
    z_dn = along_z(7)

    def load(source, target, i):
        copy = pltpu.make_async_copy(source, target, in_sem.at[i])
        copy.start()
        return copy

    acts_load = load(acts_h, acts, 0)
    txt_load = load(txt_h, txt_in, 1)
    img_load = load(img_h, img_in.at[:, pl.ds(0, D)], 2)
    wup_load = load(wup_h, wup, 3)
    cot_load = load(cot_h, cot, 4)
    wdn_load = load(wdn_h, wdn, 5)

    barrier = pltpu.get_barrier_semaphore()
    partners = [near(s) for s in (2, 4, 6, -2, -4, -6)]
    partners += [(sibling, mp), special, (me, 1 - mp)]
    partners += [along_z(q) for q in range(1, 8)]
    partners += [in_plane(q, to) for q in range(1, 8) for to in (core, 1 - core)]
    for partner in partners:
        pl.semaphore_signal(barrier, inc=1, device_id=partner, device_id_type=MESH)

    def send(source, target, send_sem, recv_sem, device):
        copy = pltpu.make_async_remote_copy(
            src_ref=source,
            dst_ref=target,
            send_sem=send_sem,
            recv_sem=recv_sem,
            device_id=device,
            device_id_type=MESH,
        )
        copy.start()
        pending.append(copy)

    def arrived(target, send_sem, recv_sem):
        pltpu.make_async_remote_copy(
            src_ref=target,
            dst_ref=target,
            send_sem=send_sem,
            recv_sem=recv_sem,
            device_id=(sibling, mp),
            device_id_type=MESH,
        ).wait_recv()

    pending = []

    txt_load.wait()

    @pl.loop(0, TXTS // LN)
    def _(i):
        r = rows(i * LN, LN)
        full = txt_in[r, :].astype(F32)
        norm = jnp.sqrt(jnp.sum(full * full, axis=-1, keepdims=True) + EPS)
        unit = full / norm
        txt_unit[r, :] = unit
        txt_norm[r, :] = jnp.broadcast_to(norm, (LN, 128))
        own_texts[r, :] = unit.astype(BF16)

    img_load.wait()

    @pl.loop(0, IMGS // LN)
    def _(i):
        r = rows(i * LN, LN)
        full = img_in[r, 0:D].astype(F32)
        norm = jnp.sqrt(jnp.sum(full * full, axis=-1, keepdims=True) + EPS)
        unit = full / norm
        img_unit[r, :] = unit
        img_norm[r, :] = jnp.broadcast_to(norm, (LN, 128))
        images[0, r, 0:D] = unit.astype(BF16)

    texts[0] = own_texts[rows(mp * HTXT, HTXT), :]

    mark_row = lax.broadcasted_iota(jnp.int32, (IMGS, IMGS), 0)
    mark_col = lax.broadcasted_iota(jnp.int32, (IMGS, IMGS), 1)
    marks = jnp.where(mark_row == 0, pstep[...], prow[...]).astype(F32).astype(BF16)
    for place in (0, IMGS):
        images[0, :, D + place : D + place + IMGS] = marks
        img_in[:, D + place : D + place + IMGS] = marks

    acts_load.wait()

    @pl.loop(0, TOK // LN)
    def _(i):
        r = rows(i * LN, LN)
        full = acts[r, :].astype(F32)
        mean = jnp.mean(full, axis=-1, keepdims=True)
        centred = full - mean
        scale = lax.rsqrt(jnp.mean(centred * centred, axis=-1, keepdims=True) + EPS)
        out = centred * scale
        normed[r, :] = out
        rstd[r, :] = jnp.broadcast_to(scale, (LN, 128))
        pair_l[core, r, :] = out.astype(BF16)

    cot_load.wait()

    @pl.loop(0, TOK // LN)
    def _(i):
        r = rows(i * LN, LN)
        pair_l[1 - core, r, :] = cot[r, :]

    pl.semaphore_wait(barrier, len(partners))

    send(pair_l.at[1], left_in, pair_ss.at[0], pair_rs.at[0], (sibling, mp))

    send(img_in, img_too, pair_ss.at[3], pair_rs.at[3], (me, 1 - mp))
    for i in (1, 3):
        send(texts.at[0], texts.at[2 * i], text_ss.at[i], text_rs.at[i], near(2 * i))
        send(images.at[0], images.at[2 * i], img_ss.at[i], img_rs.at[i], near(-2 * i))
    text_special = (
        (1 - core) * sibling + core * special[0],
        (1 - core) * mp + core * special[1],
    )
    img_special = (
        core * sibling + (1 - core) * special[0],
        core * mp + (1 - core) * special[1],
    )
    send(texts.at[0], texts.at[1 + 6 * core], text_ss.at[0], text_rs.at[0], text_special)
    send(images.at[0], images.at[7 - 6 * core], img_ss.at[0], img_rs.at[0], img_special)

    wup_load.wait()
    wdn_load.wait()

    def hidden_tile(start, width):
        c = pl.ds(start, width)
        pre = nn_dot(pair_l[core, :, :], wup[:, c])
        dhidden = nn_dot(cot[...], wdn[:, c])
        square = pre * pre
        t = jnp.tanh(GELU_C * (pre + GELU_A * (square * pre)))
        half = 0.5 * (1.0 + t)
        slope = half + (0.5 * GELU_C) * pre * (1.0 - t * t) * (1.0 + (3.0 * GELU_A) * square)
        pair_r[1 - core, :, c] = (pre * half).astype(BF16)
        pair_r[core, :, c] = (dhidden * slope).astype(BF16)

    wide_tiles(hidden_tile)
    send(pair_r.at[1], right_in, pair_ss.at[1], pair_rs.at[1], (sibling, mp))

    def dnorm_tile(start, width):
        c = pl.ds(start, width)
        dnorm[:, c] = nt_dot(pair_r[core, :, :], wup[c, :])

    wide_tiles(dnorm_tile)

    @pl.loop(0, TOK // LN)
    def _(i):
        r = rows(i * LN, LN)
        value = dnorm[r, :]
        unit = normed[r, :]
        inner = (
            value
            - jnp.mean(value, axis=-1, keepdims=True)
            - unit * jnp.mean(value * unit, axis=-1, keepdims=True)
        )
        inner_out[r, :] = inner.astype(BF16)

    send(inner_out, inner_in, inner_ss, inner_rs, (me, 1 - mp))

    def hand_on(i):
        send(
            texts.at[2 * i],
            texts.at[2 * i + 1 - 2 * core],
            text_ss.at[3 + i],
            text_rs.at[3 + i],
            (sibling, mp),
        )
        send(
            images.at[2 * i],
            images.at[2 * i - 1 + 2 * core],
            img_ss.at[3 + i],
            img_rs.at[3 + i],
            (sibling, mp),
        )

    arrived(texts.at[2], text_ss.at[1], text_rs.at[1])
    send(texts.at[2], texts.at[4], text_ss.at[2], text_rs.at[2], near(2))
    arrived(images.at[2], img_ss.at[1], img_rs.at[1])
    send(images.at[2], images.at[4], img_ss.at[2], img_rs.at[2], near(-2))
    hand_on(1)

    arrived(left_in, pair_ss.at[0], pair_rs.at[0])
    arrived(right_in, pair_ss.at[1], pair_rs.at[1])

    def grad_tile(start, width):
        c = pl.ds(start, width)
        grads[c, :] = tn_dot(pair_l[0, :, c], pair_r[0]) + tn_dot(left_in[:, c], right_in[...])

    wide_tiles(grad_tile)

    def hop(s, c, shift, out, came, ss, rs, device):
        base = ((zpos + shift) % NZ) * ZROWS
        part = pl.ds(c * SUB, SUB)
        value = grads[rows(base + c * SUB, SUB), 0:CZ]
        if s > 0:
            arrived(came.at[s - 1, part], ss.at[s - 1, c], rs.at[s - 1, c])
            value = value + came[s - 1, part, :].astype(F32)
        out[s, part, :] = value.astype(BF16)
        send(out.at[s, part], came.at[s, part], ss.at[s, c], rs.at[s, c], device)

    def x_term(shift, c):
        there = (xpos + shift) % NX
        return jnp.concatenate(
            [
                grads[rows(144 * z + 72 * h + 16 * there, HWIN, 8), CZ:]
                for z in (2 * c, 2 * c + 1)
                for h in (0, 1)
            ],
            axis=0,
        )

    def x_hop(s, c, shift, out, came, ss, rs, device, add):
        part = pl.ds(c * XSUB, XSUB)
        value = x_term(shift, c)
        if add:
            arrived(came.at[0, part], ss.at[0, c], rs.at[0, c])
            value = value + came[0, part, :].astype(F32)
        out[s, part, :] = value.astype(BF16)
        send(out.at[s, part], came.at[s, part], ss.at[s, c], rs.at[s, c], device)

    def x_down(s, c, shift, add=False):
        x_hop(s, c, shift, xd_out, xd_in, xd_ss, xd_rs, x_dn, add)

    def x_over(s, c, shift, add=False):
        x_hop(s, c, shift, xu_out, xu_in, xu_ss, xu_rs, x_up, add)

    def z_step(s):
        for c in range(NSUB):
            hop(s, c, 4 - s, up_out, up_in, up_ss, up_rs, z_up)
            if s < 3:
                hop(s, c, 5 + s, dn_out, dn_in, dn_ss, dn_rs, z_dn)

    z_step(0)

    x_down(0, 0, 2)
    x_over(0, 2, 2)
    x_down(0, 1, 2)
    x_over(0, 3, 2)
    for c in (2, 3):
        x_down(1, c, 3)
        x_over(1, c - 2, 1)

    z_step(1)

    for c in (0, 1):
        x_down(1, c, 3, True)
        x_over(1, c + 2, 1, True)

    for i in (3, 2):
        arrived(texts.at[2 * i], text_ss.at[i], text_rs.at[i])
        arrived(images.at[2 * i], img_ss.at[i], img_rs.at[i])
        hand_on(i)

    z_step(2)

    arrived(texts.at[7 - 6 * core], text_ss.at[0], text_rs.at[0])
    arrived(images.at[1 + 6 * core], img_ss.at[0], img_rs.at[0])
    for i in (1, 2, 3):
        arrived(texts.at[2 * i - 1 + 2 * core], text_ss.at[3 + i], text_rs.at[3 + i])
        arrived(images.at[2 * i + 1 - 2 * core], img_ss.at[3 + i], img_rs.at[3 + i])

    scale = scale_ref[0]
    bias = bias_ref[0]

    def slope_of(logits, positive):
        label = jnp.where(positive, 1.0, -1.0).astype(F32)
        return (-label * jax.nn.sigmoid(-label * logits)).astype(BF16)

    def target_of(marked):
        return marked[0:1, :] * float(TXTS) + marked[1:2, :]

    def project(value, unit, norm):
        return (value - unit * jnp.sum(unit * value, axis=-1, keepdims=True)) / norm

    words = own_texts[...]
    text_ids = lax.broadcasted_iota(jnp.int32, (TXTS, 128), 0).astype(F32)
    second = (lax.broadcasted_iota(jnp.int32, (TXTS, 128), 1) // IMGS).astype(F32)
    lane_second = lax.broadcasted_iota(jnp.int32, (16, 128), 1) >= IMGS
    dtxt = jnp.zeros((TXTS, D), F32)
    for pair in range(STEPS // 2):
        block = images[2 * pair : 2 * pair + 2, :, 0:D].reshape(2 * IMGS, D)
        logits = scale * nt_dot(words, block) + bias
        first = images[2 * pair, 0:16, D : D + META].astype(F32)
        later = images[2 * pair + 1, 0:16, D : D + META].astype(F32)
        target = target_of(jnp.where(lane_second, later, first))
        positive = target == (text_ids + (second + float(2 * pair)) * float(TXTS))
        dtxt = dtxt + nn_dot(slope_of(logits, positive), block)
    gt_out[...] = project(scale * dtxt, txt_unit[...], txt_norm[:, 0:1]).astype(BF16)
    send(gt_out, gt_in, pair_ss.at[2], pair_rs.at[2], (me, 1 - mp))

    z_step(3)

    for turn in (2, 1, 3, 0):
        c = (zpos // 2 + turn) % NXSUB
        part = rows(c * XSUB, XSUB)
        arrived(xd_in.at[1, part], xd_ss.at[1, c], xd_rs.at[1, c])
        arrived(xu_in.at[1, part], xu_ss.at[1, c], xu_rs.at[1, c])
        value = x_term(0, c) + xd_in[1, part, :].astype(F32) + xu_in[1, part, :].astype(F32)
        xsum[part, :] = value
        xsum_bf[part, :] = value.astype(BF16)
        for there in ((2 * c, 2 * c + 1) if turn else (zpos + 1 - 2 * (zpos % 2),)):
            send(
                xsum_bf.at[rows(there * ZWIN, ZWIN)],
                zwin_in.at[zpos],
                zwin_ss.at[there],
                zwin_rs.at[zpos],
                along_z((there - zpos + NZ) % NZ),
            )

    arrived(img_too, pair_ss.at[3], pair_rs.at[3])
    full = img_too[:, 0:D].astype(F32)
    norm = jnp.sqrt(jnp.sum(full * full, axis=-1, keepdims=True) + EPS)
    unit = full / norm
    img_unit[IMGS:, :] = unit
    img_norm[IMGS:, :] = jnp.broadcast_to(norm, (IMGS, 128))
    both[0:IMGS, :] = images[0, :, 0:D]
    both[IMGS:, :] = unit.astype(BF16)

    def as_column(marked):
        line = target_of(marked.astype(F32))[:, 0:IMGS]
        return jnp.sum(jnp.where(mark_row == mark_col, line, 0.0), axis=-1, keepdims=True)

    want = jnp.concatenate(
        [as_column(img_in[0:16, D : D + META]), as_column(img_too[0:16, D : D + META])], axis=0
    )
    lane = lax.broadcasted_iota(jnp.int32, (2 * IMGS, 2 * HTXT), 1)
    pictures = both[...]
    dimg = jnp.zeros((2 * IMGS, D), F32)
    for pair in range(STEPS // 2):
        block = texts[2 * pair : 2 * pair + 2].reshape(2 * HTXT, D)
        starts = [k * TXTS + near(-k)[1] * HTXT for k in (2 * pair, 2 * pair + 1)]
        column = jnp.where(lane < HTXT, lane + starts[0], lane + (starts[1] - HTXT))
        logits = scale * nt_dot(pictures, block) + bias
        dimg = dimg + nn_dot(slope_of(logits, want == column.astype(F32)), block)
    dimg = project(scale * dimg, img_unit[...], img_norm[:, 0:1])
    gimg[...] = dimg[0:IMGS, :]
    gi_out[...] = dimg[IMGS:, :].astype(BF16)
    send(gi_out, gi_in, pair_ss.at[4], pair_rs.at[4], (me, 1 - mp))

    arrived(inner_in, inner_ss, inner_rs)

    @pl.loop(0, TOK // LN)
    def _(i):
        r = rows(i * LN, LN)
        total = inner_out[r, :].astype(F32) + inner_in[r, :].astype(F32)
        gacts[r, :] = (cot[r, :].astype(F32) + rstd[r, 0:1] * total).astype(BF16)

    stores = [load(gacts, gacts_h, 6)]

    base = zpos * ZROWS
    for c in range(NSUB):
        part = pl.ds(c * SUB, SUB)
        arrived(up_in.at[3, part], up_ss.at[3, c], up_rs.at[3, c])
        arrived(dn_in.at[2, part], dn_ss.at[2, c], dn_rs.at[2, c])
        value = (
            grads[rows(base + c * SUB, SUB), 0:CZ]
            + up_in[3, part, :].astype(F32)
            + dn_in[2, part, :].astype(F32)
        )
        zsum[part, :] = value
    zsum[ZROWS:, :] = jnp.zeros((16, CZ), F32)
    for there in range(8):
        for to in range(2):
            first = 2 * OUT * there + OUT * to
            win_out[there, to] = zsum[first : first + 16, :].astype(BF16)
    for q in (6, 2, 5, 3, 4, 7, 1, 0):
        for to in (core, 1 - core)[q == 0 :]:
            send(
                win_out.at[(plane + q) % 8, to],
                win_in.at[core, q],
                win_ss.at[to, q],
                win_rs.at[core, q],
                in_plane(q, to),
            )
    win_in[core, 0] = win_out[plane, core]

    total = xsum[rows(zpos * ZWIN, ZWIN), :]
    for q in range(1, 8):
        there = (zpos + q) % NZ
        arrived(zwin_in.at[there], zwin_ss.at[there], zwin_rs.at[there])
        total = total + zwin_in[there].astype(F32)

    parts[0:ZWIN, :] = pltpu.roll(total, (ZWIN - 2 * xpos) % ZWIN, 0)
    parts[ZWIN:, :] = jnp.zeros((16, CX), F32)
    for to_half in range(2):
        for to in range(2):
            first = HWIN * to_half + OUT * to
            y_out[to_half, to] = parts[first : first + 16, :].astype(BF16)
    for other, to in ((1, core), (1, 1 - core), (0, 1 - core)):
        send(
            y_out.at[(half + other) % 2, to],
            y_in.at[core, other],
            y_ss.at[to, other],
            y_rs.at[core, other],
            in_plane(4 * other, to),
        )
    y_in[core, 0] = y_out[half, core]

    arrived(gt_in, pair_ss.at[2], pair_rs.at[2])
    gtxt[...] = gt_out[...].astype(F32) + gt_in[...].astype(F32)
    arrived(gi_in, pair_ss.at[4], pair_rs.at[4])
    gimg[...] = gimg[...] + gi_in[...].astype(F32)
    stores.append(load(gtxt, gtxt_h, 7))
    stores.append(load(gimg, gimg_h, 8))

    arrived(win_in.at[1 - core, 0], win_ss.at[1 - core, 0], win_rs.at[1 - core, 0])
    arrived(y_in.at[1 - core, 0], y_ss.at[1 - core, 0], y_rs.at[1 - core, 0])
    for origin, result in ((0, gup), (1, gdn)):
        total = win_in[origin, 0].astype(F32)
        for q in range(1, 8):
            arrived(win_in.at[origin, q], win_ss.at[origin, q], win_rs.at[origin, q])
            total = total + win_in[origin, q].astype(F32)
        result[:, 0:CZ] = total[0:OUT, :]
    for origin, result in ((0, gup), (1, gdn)):
        arrived(y_in.at[origin, 1], y_ss.at[origin, 1], y_rs.at[origin, 1])
        total = y_in[origin, 0].astype(F32) + y_in[origin, 1].astype(F32)
        result[:, CZ:] = total[0:OUT, :]
    stores.append(load(gup, gup_h, 9))
    stores.append(load(gdn, gdn_h, 10))
    for store in stores:
        store.wait()

    for copy in pending:
        copy.wait_send()


def hand_over(*refs):
    sources, targets, held, sems = refs[0:5], refs[5:10], refs[10:15], refs[15]
    order = (4, 1, 0, 2, 3)
    into = [pltpu.make_async_copy(sources[i], held[i], sems.at[0, i]) for i in order]
    onto = [pltpu.make_async_copy(held[i], targets[i], sems.at[1, i]) for i in order]
    for copy in into:
        copy.start()
    for copy, after in zip(into, onto):
        copy.wait()
        after.start()
    for after in onto:
        after.wait()


def shards(
    img_emb, txt_emb, logit_scale, logit_bias, pos_step, pos_row, acts, cotangent, w_up, w_down
):
    pstep = pos_step.reshape(1, IMGS)
    prow = pos_row.reshape(1, IMGS)
    vmem = pl.BlockSpec(memory_space=pltpu.VMEM)
    smem = pl.BlockSpec(memory_space=pltpu.SMEM)
    hbm = pl.BlockSpec(memory_space=pl.ANY)
    dma = pltpu.SemaphoreType.DMA
    out = pl.pallas_call(
        step_kernel,
        out_shape=(
            jax.ShapeDtypeStruct((IMGS, D), F32),
            jax.ShapeDtypeStruct((TXTS, D), F32),
            jax.ShapeDtypeStruct((OUT, HALF), F32),
            jax.ShapeDtypeStruct((OUT, HALF), F32),
            jax.ShapeDtypeStruct((TOK, D), BF16),
        ),
        in_specs=[smem, smem, hbm, hbm, vmem, vmem, hbm, hbm, hbm, hbm],
        out_specs=(hbm, hbm, hbm, hbm, hbm),
        scratch_shapes=[
            pltpu.VMEM((IMGS, D), F32),
            pltpu.VMEM((TXTS, D), F32),
            pltpu.VMEM((OUT, HALF), F32),
            pltpu.VMEM((OUT, HALF), F32),
            pltpu.VMEM((TOK, D), BF16),
            pltpu.VMEM((IMGS, D + META), BF16),
            pltpu.VMEM((TXTS, D), BF16),
            pltpu.VMEM((TOK, D), BF16),
            pltpu.VMEM((TOK, D), BF16),
            pltpu.VMEM((D, HALF), BF16),
            pltpu.VMEM((D, HALF), BF16),
            pltpu.VMEM((2, TOK, D), BF16),
            pltpu.VMEM((2, TOK, HALF), BF16),
            pltpu.VMEM((TOK, D), BF16),
            pltpu.VMEM((TOK, HALF), BF16),
            pltpu.VMEM((TOK, D), F32),
            pltpu.VMEM((TOK, 128), F32),
            pltpu.VMEM((TOK, D), F32),
            pltpu.VMEM((D, HALF), F32),
            pltpu.VMEM((4, ZROWS, CZ), BF16),
            pltpu.VMEM((4, ZROWS, CZ), BF16),
            pltpu.VMEM((3, ZROWS, CZ), BF16),
            pltpu.VMEM((3, ZROWS, CZ), BF16),
            pltpu.VMEM((TOK, D), BF16),
            pltpu.VMEM((TOK, D), BF16),
            pltpu.VMEM((2, XROWS, CX), BF16),
            pltpu.VMEM((2, XROWS, CX), BF16),
            pltpu.VMEM((2, XROWS, CX), BF16),
            pltpu.VMEM((2, XROWS, CX), BF16),
            pltpu.VMEM((ZROWS + 16, CZ), F32),
            pltpu.VMEM((XROWS, CX), F32),
            pltpu.VMEM((XROWS, CX), BF16),
            pltpu.VMEM((8, 2, 16, CZ), BF16),
            pltpu.VMEM((2, 8, 16, CZ), BF16),
            pltpu.VMEM((NZ, ZWIN, CX), BF16),
            pltpu.VMEM((2, 2, 16, CX), BF16),
            pltpu.VMEM((2, 2, 16, CX), BF16),
            pltpu.VMEM((ZWIN + 16, CX), F32),
            pltpu.VMEM((TXTS, D), BF16),
            pltpu.VMEM((STEPS, HTXT, D), BF16),
            pltpu.VMEM((STEPS, IMGS, D + META), BF16),
            pltpu.VMEM((IMGS, D + META), BF16),
            pltpu.VMEM((2 * IMGS, D), BF16),
            pltpu.VMEM((TXTS, D), F32),
            pltpu.VMEM((TXTS, 128), F32),
            pltpu.VMEM((2 * IMGS, D), F32),
            pltpu.VMEM((2 * IMGS, 128), F32),
            pltpu.VMEM((TXTS, D), BF16),
            pltpu.VMEM((TXTS, D), BF16),
            pltpu.VMEM((IMGS, D), BF16),
            pltpu.VMEM((IMGS, D), BF16),
            dma((11,)),
            dma((7,)),
            dma((7,)),
            dma((7,)),
            dma((7,)),
            dma((5,)),
            dma((5,)),
            dma((4, NSUB)),
            dma((4, NSUB)),
            dma((3, NSUB)),
            dma((3, NSUB)),
            dma,
            dma,
            dma((2, NXSUB)),
            dma((2, NXSUB)),
            dma((2, NXSUB)),
            dma((2, NXSUB)),
            dma((2, 8)),
            dma((2, 8)),
            dma((NZ,)),
            dma((NZ,)),
            dma((2, 2)),
            dma((2, 2)),
        ],
        compiler_params=pltpu.CompilerParams(
            collective_id=0, has_side_effects=True, vmem_limit_bytes=58 * 1024 * 1024
        ),
        name="step",
    )(logit_scale, logit_bias, img_emb, txt_emb, pstep, prow, acts, cotangent, w_up, w_down)
    return pl.pallas_call(
        hand_over,
        out_shape=tuple(jax.ShapeDtypeStruct(x.shape, x.dtype) for x in out),
        in_specs=[hbm] * 5,
        out_specs=(hbm,) * 5,
        scratch_shapes=[pltpu.VMEM(x.shape, x.dtype) for x in out] + [dma((2, 5))],
        name="hand_over",
    )(*out)


def solution(mesh):
    return jax.shard_map(
        shards,
        mesh=mesh,
        in_specs=(
            P(("dp", "mp"), None),
            P("dp", None),
            P(),
            P(),
            P(("dp", "mp")),
            P(("dp", "mp")),
            P("dp", None),
            P("dp", None),
            P(None, "mp"),
            P(None, "mp"),
        ),
        out_specs=(
            P(("dp", "mp"), None),
            P("dp", None),
            P("dp", "mp"),
            P("dp", "mp"),
            P("dp", None),
        ),
        check_vma=False,
    )
```
